32 devices in a mesh: lat: 16 (over z, y, x), lon: 2 (over core).
Axes of the slice: x: 2, y: 2, z: 4, core: 2. Of those that a mesh axis runs over, the one named last changes fastest.
Arguments:
- velocity: float32 [2, 8, 128, 256], P(None, None, 'lat', 'lon'), may hold values from -1.8 to 1.8
- thickness: float32 [8, 128, 256], P(None, 'lat', 'lon'), may hold values from 0.5 to 1.5
- hydrography: float32 [2, 8, 128, 256], P(None, None, 'lat', 'lon'), may hold values from -6 to 6
- tracers: float32 [17, 8, 128, 256], P(None, None, 'lat', 'lon'), may hold values from -6 to 6
- land_mask: int32 [128, 256], P('lat', 'lon'), may hold values 0 or 1
- bottom_layer: int32 [128, 256], P('lat', 'lon'), may hold values from 1 to 8
- row_biome: int32 [128], P('lat'), may hold values from 0 to 3
- reaction_rates: float32 [17, 17], replicated, may hold values from -0.75 to 0.75
- growth_rates: float32 [4], replicated, may hold values from 0.2 to 2
Outputs:
- new_velocity: float32 [2, 8, 128, 256], P(None, None, 'lat', 'lon')
- new_thickness: float32 [8, 128, 256], P(None, 'lat', 'lon')
- new_hydrography: float32 [2, 8, 128, 256], P(None, None, 'lat', 'lon')
- new_tracers: float32 [17, 8, 128, 256], P(None, None, 'lat', 'lon')
- absorbed: float32 [8, 128, 256], P(None, 'lat', 'lon')
The draws below stay inside these ranges and needn't reach their ends.
All inputs are finite; a program needn't handle non-finite values. No bound on the sum of `land_mask` on one device may be relied on, other than what follows from the above.
Results may differ from the reference program's by a relative error of at most 0.0003.
Values sent between devices are 32-bit elements; how exact they have to be, the bound alone decides.
A program may use at most 64 MiB of HBM per device.

```python
import math
import jax
import jax.numpy as jnp
from jax import lax

NTR = 17
NBIOME = 4
NSUB = 2
K = 8
NY = 128
NX = 256


def set_ends(drawn, key, least, high):
    index_at = [jax.random.randint(jax.random.fold_in(key, axis), (), 0, length) for axis, length in enumerate(drawn.shape)]
    longest = drawn.shape.index(max(drawn.shape))
    beside = index_at[:longest] + [(index_at[longest] + 1) % drawn.shape[longest]] + index_at[longest + 1:]
    return drawn.at[tuple(index_at)].set(least).at[tuple(beside)].set(high)


def block_levels(key, dims, pieces, smallest, high):
    factor_of, own = 1.0, jax.random.fold_in(key, 6)
    for position, shards_of in pieces:
        steps = jnp.exp(jax.random.uniform(jax.random.fold_in(own, position), (shards_of,), jnp.float32, smallest / len(pieces), high / len(pieces)))
        factor_of = factor_of * jnp.repeat(steps, dims[position] // shards_of).reshape([-1 if axis == position else 1 for axis in range(len(dims))])
    return factor_of


def gaussian(key, extent, scale, most, shards=(), dtype=jnp.bfloat16):
    drawn = scale * jax.random.normal(key, extent, jnp.float32)
    if shards:
        drawn = drawn * block_levels(key, extent, shards, -0.22, 0.18)
    return jnp.clip(drawn, -most, most).astype(dtype)


def setup_inputs(seed: int = 0) -> dict:
    splits = jax.random.split(jax.random.key(seed), 10)
    return {
        "velocity": gaussian(splits[0], (2, K, NY, NX), 0.3, 1.8, ((2, 16), (3, 2)), jnp.float32),
        "thickness": jnp.clip(0.5 + 1.0 * jax.random.uniform(splits[1], (K, NY, NX), jnp.float32) ** block_levels(splits[1], (K, NY, NX), ((1, 16), (2, 2)), -0.2, 0.2), 0.5, 1.5),
        "hydrography": gaussian(splits[2], (2, K, NY, NX), 1.0, 6.0, ((2, 16), (3, 2)), jnp.float32),
        "tracers": gaussian(splits[3], (NTR, K, NY, NX), 1.0, 6.0, ((2, 16), (3, 2)), jnp.float32),
        "land_mask": set_ends((jax.random.randint(splits[4], (NY, NX), 0, 4) < 3).astype(jnp.int32), jax.random.fold_in(splits[4], 1), 0, 1),
        "bottom_layer": set_ends(jax.random.randint(splits[5], (NY, NX), 1, K + 1), jax.random.fold_in(splits[5], 1), 1, K).astype(jnp.int32),
        "row_biome": set_ends(jax.random.randint(splits[6], (NY,), 0, NBIOME), jax.random.fold_in(splits[6], 1), 0, NBIOME - 1).astype(jnp.int32),
        "reaction_rates": gaussian(splits[7], (NTR, NTR), (4 * NTR) ** -0.5, 0.75, (), jnp.float32),
        "growth_rates": jnp.clip(jnp.exp(jax.random.uniform(splits[8], (NBIOME,), jnp.float32, math.log(0.2), math.log(2.0))), 0.2, 2.0),
    }


heat_coef = 0.2
salt_coef = 0.25
gravity = 0.3
viscosity = 0.1
coriolis_coef = 0.3
tracer_diff = 0.1
kappa_base = 0.02
kappa_var = 0.1
water_att = 0.1
chlorophyll_att = 0.2
heat_gain = 1.0


def shifted(values, step_rows, step_cols):
    leading = [(0, 0)] * (values.ndim - 2)
    padded = jnp.pad(values, leading + [(1, 1), (1, 1)])
    height_span = values.shape[-2]
    width_span = values.shape[-1]
    return padded[..., 1 + step_rows:1 + step_rows + height_span, 1 + step_cols:1 + step_cols + width_span]


def face_masks(wet_cells):
    return wet_cells * shifted(wet_cells, 0, 1), wet_cells * shifted(wet_cells, 1, 0)


def laplace(values, wet_east, wet_north):
    east_flux = wet_east * (shifted(values, 0, 1) - values)
    north_flux = wet_north * (shifted(values, 1, 0) - values)
    return east_flux - shifted(east_flux, 0, -1) + north_flux - shifted(north_flux, -1, 0)


def wet_layers(floor_depth, layers):
    layer_height = lax.broadcasted_iota(jnp.float32, (layers, 1, 1), 0)
    return (layer_height < floor_depth[None]).astype(jnp.float32)


def latitude_rows(start, count, total_rows):
    positions = start + lax.broadcasted_iota(jnp.float32, (count, 1), 0)
    return 2.0 * (positions + 0.5) / total_rows - 1.0


def density_of(hydrography):
    return salt_coef * hydrography[1] - heat_coef * hydrography[0]


def momentum(velocity, thickness, hydrography, wet_cells, coriolis):
    flow_east = velocity[0]
    flow_north = velocity[1]
    wet_east, wet_north = face_masks(wet_cells)
    pressure = gravity * thickness + density_of(hydrography)
    new_east = wet_east * (flow_east + coriolis * flow_north - (shifted(pressure, 0, 1) - pressure) + viscosity * laplace(flow_east, wet_east, wet_north))
    new_north = wet_north * (flow_north - coriolis * flow_east - (shifted(pressure, 1, 0) - pressure) + viscosity * laplace(flow_north, wet_east, wet_north))
    volume_east = wet_east * flow_east * 0.5 * (thickness + shifted(thickness, 0, 1))
    volume_north = wet_north * flow_north * 0.5 * (thickness + shifted(thickness, 1, 0))
    new_height = wet_cells * (thickness - (volume_east - shifted(volume_east, 0, -1) + volume_north - shifted(volume_north, -1, 0)))
    return new_east, new_north, new_height


def mixing(hydrography, wet_cells):
    density = density_of(hydrography)
    below = jnp.concatenate([density[1:] - density[:-1], jnp.zeros((1,) + density.shape[1:], jnp.float32)], 0)
    return wet_cells * (kappa_base + kappa_var / (1.0 + 10.0 * below * below))


def heat_salt(hydrography, wet_cells):
    wet_east, wet_north = face_masks(wet_cells)
    return wet_cells * (hydrography + tracer_diff * laplace(hydrography, wet_east, wet_north))


def light_field(tracers, wet_cells, insolation):
    chlorophyll = tracers[1]
    attenuation = wet_cells * (water_att + chlorophyll_att * chlorophyll * chlorophyll)
    overhead = jnp.cumsum(attenuation, axis=0) - attenuation
    top_light = insolation * jnp.exp(-overhead)
    return top_light, top_light * (1.0 - jnp.exp(-attenuation))


def tracer_step(tracers, flow_east, flow_north, thickness, kappa, wet_cells, reaction_rates, growth_field, top_light):
    sub_step = 1.0 / NSUB
    wet_east, wet_north = face_masks(wet_cells)
    transport_x = wet_east * flow_east * 0.5 * (thickness + shifted(thickness, 0, 1))
    transport_y = wet_north * flow_north * 0.5 * (thickness + shifted(thickness, 1, 0))
    diffuse_x = wet_east * 0.5 * (kappa + shifted(kappa, 0, 1))
    diffuse_y = wet_north * 0.5 * (kappa + shifted(kappa, 1, 0))
    east_next = shifted(tracers, 0, 1)
    north_next = shifted(tracers, 1, 0)
    flux_x = transport_x * jnp.where(transport_x > 0, tracers, east_next) - diffuse_x * (east_next - tracers)
    flux_y = transport_y * jnp.where(transport_y > 0, tracers, north_next) - diffuse_y * (north_next - tracers)
    advected = tracers - sub_step * (flux_x - shifted(flux_x, 0, -1) + flux_y - shifted(flux_y, -1, 0))
    flattened = advected.reshape(advected.shape[0], -1)
    coupled = jnp.dot(reaction_rates, flattened, precision=lax.Precision.HIGHEST).reshape(advected.shape)
    nutrient = advected[0]
    plankton = advected[1]
    uptake = growth_field * top_light * plankton * nutrient * nutrient / (1.0 + nutrient * nutrient)
    change = jnp.concatenate([(coupled[0] - uptake)[None], (coupled[1] + uptake)[None], coupled[2:]], 0)
    return wet_cells * (advected + sub_step * change)


def reference(velocity, thickness, hydrography, tracers, land_mask, bottom_layer, row_biome, reaction_rates, growth_rates):
    floor_depth = (land_mask * bottom_layer).astype(jnp.float32)
    wet_cells = wet_layers(floor_depth, K)
    latitude = latitude_rows(jnp.float32(0.0), NY, NY)
    insolation = 1.0 - 0.8 * latitude * latitude
    coriolis = coriolis_coef * latitude
    top_light, absorbed = light_field(tracers, wet_cells, insolation)
    new_east, new_north, new_height = momentum(velocity, thickness, hydrography, wet_cells, coriolis)
    kappa = mixing(hydrography, wet_cells)
    mixed = heat_salt(hydrography, wet_cells)
    new_hydrography = jnp.concatenate([(mixed[0] + heat_gain * absorbed)[None], mixed[1:]], 0)
    biome_table = (row_biome[:, None] == lax.broadcasted_iota(jnp.int32, (1, NBIOME), 1)).astype(jnp.float32)
    growth_field = jnp.dot(biome_table, growth_rates[:, None], precision=lax.Precision.HIGHEST)
    current = tracers
    for substep in range(NSUB):
        current = tracer_step(current, new_east, new_north, new_height, kappa, wet_cells, reaction_rates, growth_field, top_light)
    return jnp.stack([new_east, new_north]), new_height, new_hydrography, current, absorbed
```

```python
import functools

import jax
import jax.numpy as jnp
from jax import lax
from jax.experimental import pallas as pl
from jax.experimental.pallas import tpu as pltpu
from jax.sharding import PartitionSpec as P

NSUB = 2
heat_coef = 0.2
salt_coef = 0.25
gravity = 0.3
viscosity = 0.1
coriolis_coef = 0.3
tracer_diff = 0.1
kappa_base = 0.02
kappa_var = 0.1
water_att = 0.1
chlorophyll_att = 0.2
heat_gain = 1.0
MESH = pl.DeviceIdType.MESH


def growth_of(biome, growth, row, kinds):
    value = jnp.float32(0.0)
    for kind in range(kinds):
        value = jnp.where(biome[row] == kind, growth[kind], value)
    return value


def write_misc(misc, land, bottom, biome, growth, rows, cols, kinds):
    misc[0:rows, :] = (land[...] * bottom[...]).astype(jnp.float32)
    for row in range(rows):
        misc[rows + row : rows + row + 1, :] = jnp.full(
            (1, cols), growth_of(biome, growth, row, kinds), jnp.float32
        )


def exchange(sizes, biome, growth, vel, thick, hydro, tracers, land, bottom, *refs):
    lats, lons, layers, rows, cols, kinds, near, sides = sizes
    fields = tracers.shape[0] // rows
    got_ns = refs[0]
    got_lon = [refs[1 + 6 * i : 7 + 6 * i] for i in range(sides)]
    misc, pack, send_ns, recv_ns, send_lon, recv_lon = refs[1 + 6 * sides :]
    lat, lon = lax.axis_index("lat"), lax.axis_index("lon")
    barrier = pltpu.get_barrier_semaphore()
    around = [
        (lat > 0, (lat - 1, lon)),
        (lat < lats - 1, (lat + 1, lon)),
        (lon > 0, (lat, lon - 1)),
        (lon < lons - 1, (lat, lon + 1)),
    ]
    for there, where in around:

        @pl.when(there)
        def _(where=where):
            pl.semaphore_signal(barrier, inc=1, device_id=where, device_id_type=MESH)

    write_misc(misc, land, bottom, biome, growth, rows, cols, kinds)

    def state_row(side, start, row):
        for ref, count in ((vel, 2 * layers), (thick, layers), (hydro, 2 * layers)):
            pack[side, start : start + count, :] = ref[pl.ds(row, count, stride=rows), :]
            start += count

    def tracer_row(side, start, row):
        pack[side, start : start + fields, :] = tracers[pl.ds(row, fields, stride=rows), :]

    state = 5 * layers
    for side in range(2):
        order = (rows - 1, rows - 2, rows - 3) if side == 0 else (0, 1, 2)
        state_row(side, 0, order[0])
        tracer_row(side, state, order[0])
        state_row(side, state + fields, order[1])
        pack[side, 2 * state + fields : near, :] = misc[...]
        tracer_row(side, near, order[1])
        state_row(side, near + fields, order[2])

    peers = sum(there.astype(jnp.int32) for there, _ in around)
    pl.semaphore_wait(barrier, peers)

    def ns_copy(side):
        to = lat + 1 if side == 0 else lat - 1
        return pltpu.make_async_remote_copy(
            src_ref=pack.at[side],
            dst_ref=got_ns.at[side],
            send_sem=send_ns.at[side],
            recv_sem=recv_ns.at[side],
            device_id=(to, lon),
            device_id_type=MESH,
        )

    def lon_copy(way, item):
        slot = way if sides == 2 else 0
        to = lon + 1 if way == 0 else lon - 1
        if item < 5:
            src = (vel, thick, hydro, tracers, misc)[item]
            dst = got_lon[slot][item]
        else:
            src = got_ns.at[item - 5, 0:near]
            dst = got_lon[slot][5].at[item - 5]
        return pltpu.make_async_remote_copy(
            src_ref=src,
            dst_ref=dst,
            send_sem=send_lon.at[way, item],
            recv_sem=recv_lon.at[way, item],
            device_id=(lat, to),
            device_id_type=MESH,
        )

    south, north = lat > 0, lat < lats - 1
    west, east = lon > 0, lon < lons - 1
    ns_send = (north, south)
    ns_recv = (south, north)
    lon_send = (east, west)
    lon_recv = (west, east)
    for side in range(2):

        @pl.when(ns_send[side])
        def _(side=side):
            ns_copy(side).start()

    for way in range(2):

        @pl.when(lon_send[way])
        def _(way=way):
            for item in range(5):
                lon_copy(way, item).start()

    for side in range(2):

        @pl.when(ns_recv[side])
        def _(side=side):
            ns_copy(side).wait_recv()
            for way in range(2):

                @pl.when(lon_send[way])
                def _(way=way):
                    lon_copy(way, 5 + side).start()

    for way in range(2):

        @pl.when(lon_recv[way])
        def _(way=way):
            for item in range(5):
                lon_copy(way, item).wait_recv()
            for side in range(2):

                @pl.when(ns_recv[side])
                def _(side=side):
                    lon_copy(way, 5 + side).wait_recv()

        @pl.when(lon_send[way])
        def _(way=way):
            for item in range(5):
                lon_copy(way, item).wait_send()
            for side in range(2):

                @pl.when(ns_recv[side])
                def _(side=side):
                    lon_copy(way, 5 + side).wait_send()

    for side in range(2):

        @pl.when(ns_send[side])
        def _(side=side):
            ns_copy(side).wait_send()


def to_east(values):
    return pltpu.roll(values, values.shape[-1] - 1, values.ndim - 1)


def to_west(values):
    return pltpu.roll(values, 1, values.ndim - 1)


def compute(sizes, biome, growth, vel, thick, hydro, tracers, land, bottom, rates, *refs):
    lats, lons, layers, rows, cols, kinds, near, sides = sizes
    fields = tracers.shape[0] // rows
    ntr = fields // layers
    got_ns = refs[0]
    got_lon = [refs[1 + 6 * i : 7 + 6 * i] for i in range(sides)]
    out_vel, out_thick, out_hydro, out_tr, out_abs = refs[1 + 6 * sides : 6 + 6 * sides]
    misc, st, tr, mid, depth, grow, coef, glow, wets = refs[6 + 6 * sides :]
    lat, lon = lax.axis_index("lat"), lax.axis_index("lon")
    span = 2 * cols
    state = 5 * layers
    write_misc(misc, land, bottom, biome, growth, rows, cols, kinds)

    lanes = lax.broadcasted_iota(jnp.int32, (1, cols), 1)
    first = lanes < cols // 2
    lane_e = jnp.logical_and(first, lon < lons - 1)
    lane_w = jnp.logical_and(jnp.logical_not(first), lon > 0)

    def beside(load, mask=None):
        west_part = load(got_lon[0])
        east_part = load(got_lon[-1])
        use_e, use_w = lane_e, lane_w
        if mask is not None:
            use_e, use_w = jnp.logical_and(use_e, mask), jnp.logical_and(use_w, mask)
        return jnp.where(use_e, east_part, jnp.where(use_w, west_part, 0.0))

    def both(ref, at, start, own, side_values):
        count = own.shape[0]
        ref[at, start : start + count, 0:cols] = own
        ref[at, start : start + count, cols:span] = side_values

    for row in range(rows):
        start = 0
        for item, (ref, count) in enumerate(
            ((vel, 2 * layers), (thick, layers), (hydro, 2 * layers))
        ):
            pick = pl.ds(row, count, stride=rows)
            both(
                st, 3 + row, start, ref[pick, :], beside(lambda got, i=item, p=pick: got[i][p, :])
            )
            start += count
        pick = pl.ds(row, fields, stride=rows)
        both(tr, 2 + row, 0, tracers[pick, :], beside(lambda got, p=pick: got[3][p, :]))
    for ref, begin in ((depth, 0), (grow, rows)):
        for row in range(rows):
            pick = slice(begin + row, begin + row + 1)
            ref[3 + row, :, 0:cols] = jnp.broadcast_to(misc[pick, :], (layers, cols))
            ref[3 + row, :, cols:span] = jnp.broadcast_to(
                beside(lambda got, p=pick: got[4][p, :]), (layers, cols)
            )
    for side in range(2):
        there = lat > 0 if side == 0 else lat < lats - 1
        mask = jnp.logical_and(lanes >= 0, there)

        def own_part(begin, count, side=side, mask=mask):
            return jnp.where(mask, got_ns[side, begin : begin + count, :], 0.0)

        def far_part(begin, count, side=side, mask=mask):
            return beside(lambda got: got[5][side, begin : begin + count, :], mask)

        place = (2, 1, 0) if side == 0 else (rows + 3, rows + 4, rows + 5)
        place_tr = (1, 0) if side == 0 else (rows + 2, rows + 3)
        source = (rows - 1, rows - 2, rows - 3) if side == 0 else (0, 1, 2)
        both(st, place[0], 0, own_part(0, state), far_part(0, state))
        both(tr, place_tr[0], 0, own_part(state, fields), far_part(state, fields))
        both(st, place[1], 0, own_part(state + fields, state), far_part(state + fields, state))
        both(tr, place_tr[1], 0, own_part(near, fields), jnp.zeros((fields, cols), jnp.float32))
        both(
            st, place[2], 0, own_part(near + fields, state), jnp.zeros((state, cols), jnp.float32)
        )
        begin = 2 * state + fields
        for ref, extra in ((depth, 0), (grow, rows)):
            for step in range(3):
                at = begin + extra + source[step]
                ref[place[step], :, 0:cols] = jnp.broadcast_to(own_part(at, 1), (layers, cols))
                ref[place[step], :, cols:span] = jnp.broadcast_to(far_part(at, 1), (layers, cols))

    total = rows * lats
    deep = rows + 6
    base = (lat * rows).astype(jnp.float32)

    def latitude(begin, count):
        at = lax.broadcasted_iota(jnp.int32, (count, layers, span), 0).astype(jnp.float32)
        return 2.0 * ((base + (at + begin)) + 0.5) / total - 1.0

    level = lax.broadcasted_iota(jnp.int32, (1, layers, span), 1)
    wet = (level.astype(jnp.float32) < depth[...]).astype(jnp.float32)
    wet_e = wet * to_east(wet)
    wet_n = wet[:-1] * wet[1:]
    u = st[:, 0:layers, :]
    v = st[:, layers : 2 * layers, :]
    h = st[:, 2 * layers : 3 * layers, :]
    warm = st[:, 3 * layers : 4 * layers, :]
    salt = st[:, 4 * layers : 5 * layers, :]

    def inner(a):
        return a[1 : deep - 1]

    def laplace(a, low, high):
        block, eface = a[low:high], wet_e[low:high]
        fe = eface * (to_east(block) - block)
        fn = wet_n[low - 1 : high] * (a[low : high + 1] - a[low - 1 : high])
        return fe - to_west(fe) + fn[1:] - fn[:-1]

    dens = salt_coef * salt - heat_coef * warm
    press = gravity * h + dens
    cor = coriolis_coef * latitude(-2.0, deep - 2)
    new_u = inner(wet_e) * (
        inner(u)
        + cor * inner(v)
        - (to_east(inner(press)) - inner(press))
        + viscosity * laplace(u, 1, deep - 1)
    )
    new_v = wet_n[1:] * (
        inner(v)
        - cor * inner(u)
        - (press[2:] - inner(press))
        + viscosity * laplace(v, 1, deep - 1)
    )
    q_e = inner(wet_e * u * 0.5 * (h + to_east(h)))
    q_n = wet_n * v[:-1] * 0.5 * (h[:-1] + h[1:])
    new_h = inner(wet) * (inner(h) - (q_e - to_west(q_e) + q_n[1:] - q_n[:-1]))
    dens = inner(dens)
    below = jnp.where(level < layers - 1, pltpu.roll(dens, layers - 1, 1) - dens, 0.0)
    kappa = inner(wet) * (kappa_base + kappa_var / (1.0 + 10.0 * below * below))

    def upwind(flow, spread):
        return jnp.maximum(flow, 0.0) + spread, jnp.minimum(flow, 0.0) - spread

    he, ke = new_h[1:-1], kappa[1:-1]
    face_e, face_n = wet_e[2:-2], wet_n[1:-1]
    a_e, b_e = upwind(
        face_e * new_u[1:-1] * 0.5 * (he + to_east(he)), face_e * 0.5 * (ke + to_east(ke))
    )
    a_n, b_n = upwind(
        face_n * new_v[:-1] * 0.5 * (new_h[:-1] + new_h[1:]),
        face_n * 0.5 * (kappa[:-1] + kappa[1:]),
    )
    sub = 1.0 / NSUB
    a_w, b_w = to_west(a_e), to_west(b_e)
    coef[0] = 1.0 - sub * (a_e - b_w + a_n[1:] - b_n[:-1])
    coef[1] = -sub * b_e
    coef[2] = sub * a_w
    coef[3] = -sub * b_n[1:]
    coef[4] = sub * a_n[:-1]
    wet_in = wet[2:-2]
    wets[...] = wet_in

    chl = tr[1 : rows + 3, layers : 2 * layers, :]
    att = wet_in * (water_att + chlorophyll_att * chl * chl)
    summed = att
    step = 1
    while step < layers:
        summed = summed + jnp.where(level >= step, pltpu.roll(summed, step, 1), 0.0)
        step *= 2
    lat_in = latitude(-1.0, rows + 2)
    top = (1.0 - 0.8 * lat_in * lat_in) * jnp.exp(att - summed)
    glow[...] = grow[2 : rows + 4] * top
    light = (top * (1.0 - jnp.exp(-att)))[1:-1, :, 0:cols]
    mine = wet[3:-3, :, 0:cols]
    mixed_t = (
        mine * (warm[3:-3] + tracer_diff * laplace(warm, 3, deep - 3))[:, :, 0:cols]
        + heat_gain * light
    )
    mixed_s = mine * (salt[3:-3] + tracer_diff * laplace(salt, 3, deep - 3))[:, :, 0:cols]
    for row in range(rows):
        pick = pl.ds(row, layers, stride=rows)
        later = pl.ds(layers * rows + row, layers, stride=rows)
        out_vel[pick, :] = new_u[2 + row, :, 0:cols]
        out_vel[later, :] = new_v[2 + row, :, 0:cols]
        out_thick[pick, :] = new_h[2 + row, :, 0:cols]
        out_hydro[pick, :] = mixed_t[row]
        out_hydro[later, :] = mixed_s[row]
        out_abs[pick, :] = light[row]

    wide = lax.broadcasted_iota(jnp.int32, (fields, ntr), 0) // layers
    pick_t = (wide == lax.broadcasted_iota(jnp.int32, (fields, ntr), 1)).astype(jnp.float32)
    spread_rates = jnp.dot(
        pick_t,
        lax.dot_general(
            rates[...],
            pick_t,
            (((1,), (1,)), ((), ())),
            precision=lax.Precision.HIGHEST,
            preferred_element_type=jnp.float32,
        ),
        precision=lax.Precision.HIGHEST,
        preferred_element_type=jnp.float32,
    )
    same = (
        lax.broadcasted_iota(jnp.int32, (fields, fields), 0) % layers
        == lax.broadcasted_iota(jnp.int32, (fields, fields), 1) % layers
    )
    couple = jnp.where(same, sub * spread_rates, 0.0)
    couple_hi = couple.astype(jnp.bfloat16)
    couple_lo = (couple - couple_hi.astype(jnp.float32)).astype(jnp.bfloat16)

    def advance(src, at, width):
        c = src[at + 1].reshape(ntr, layers, span)
        up = src[at + 2].reshape(ntr, layers, span)[:, :, 0:width]
        down = src[at].reshape(ntr, layers, span)[:, :, 0:width]
        return c, up, down

    def finish(src, at, face, width):
        c, up, down = advance(src, at, width)
        k = [coef[i, face, :, 0:width] for i in range(5)]
        adv = (
            k[0] * c[:, :, 0:width]
            + k[1] * to_east(c)[:, :, 0:width]
            + k[2] * to_west(c)[:, :, 0:width]
            + k[3] * up
            + k[4] * down
        )
        flat = adv.reshape(fields, width)
        hi = flat.astype(jnp.bfloat16)
        lo = (flat - hi.astype(jnp.float32)).astype(jnp.bfloat16)

        def mul(a, b):
            return jnp.dot(a, b, preferred_element_type=jnp.float32)

        new = flat + (mul(couple_hi, hi) + (mul(couple_hi, lo) + mul(couple_lo, hi)))
        nut, plk = adv[0], adv[1]
        uptake = glow[face, :, 0:width] * plk * nut * nut / (1.0 + nut * nut)
        new = new.reshape(ntr, layers, width)
        w = wets[face, :, 0:width]
        first_two = (
            w * (new[0] - sub * uptake),
            w * (new[1] + sub * uptake),
        )
        return (w * new).reshape(fields, width), first_two

    def first_step(at, carry):
        new, (zero, one) = finish(tr, at, at, span)
        mid[at] = new
        mid[at, 0:layers, :] = zero
        mid[at, layers : 2 * layers, :] = one
        return carry

    lax.fori_loop(0, rows + 2, first_step, 0)
    for row in range(rows):
        new, (zero, one) = finish(mid, row, row + 1, cols)
        out_tr[pl.ds(row, fields, stride=rows), :] = new
        out_tr[pl.ds(row, layers, stride=rows), :] = zero
        out_tr[pl.ds(layers * rows + row, layers, stride=rows), :] = one


def per_device(
    velocity,
    thickness,
    hydrography,
    tracers,
    land_mask,
    bottom_layer,
    row_biome,
    reaction_rates,
    growth_rates,
):
    ntr, layers, rows, cols = tracers.shape
    lats, lons = lax.axis_size("lat"), lax.axis_size("lon")
    state, fields = 5 * layers, ntr * layers
    near = 2 * state + fields + 2 * rows
    whole = near + fields + state
    sides = 1 if lons <= 2 else 2
    sizes = (lats, lons, layers, rows, cols, growth_rates.shape[0], near, sides)
    flat = [a.reshape(-1, cols) for a in (velocity, thickness, hydrography, tracers)]
    vmem = pl.BlockSpec(memory_space=pltpu.VMEM)
    smem = pl.BlockSpec(memory_space=pltpu.SMEM)
    f32 = jnp.float32
    lon_shapes = [jax.ShapeDtypeStruct(a.shape, f32) for a in flat] + [
        jax.ShapeDtypeStruct((2 * rows, cols), f32),
        jax.ShapeDtypeStruct((2, near, cols), f32),
    ]
    got = pl.pallas_call(
        functools.partial(exchange, sizes),
        out_shape=[jax.ShapeDtypeStruct((2, whole, cols), f32)] + lon_shapes * sides,
        in_specs=[smem] * 2 + [vmem] * 6,
        out_specs=[pl.BlockSpec(memory_space=pl.ANY)] * (1 + 6 * sides),
        scratch_shapes=[
            pltpu.VMEM((2 * rows, cols), f32),
            pltpu.VMEM((2, whole, cols), f32),
            pltpu.SemaphoreType.DMA((2,)),
            pltpu.SemaphoreType.DMA((2,)),
            pltpu.SemaphoreType.DMA((2, 7)),
            pltpu.SemaphoreType.DMA((2, 7)),
        ],
        compiler_params=pltpu.CompilerParams(
            collective_id=0, has_side_effects=True, vmem_limit_bytes=16 * 1024 * 1024
        ),
        name="exchange",
    )(row_biome, growth_rates, *flat, land_mask, bottom_layer)
    span = 2 * cols
    outs = pl.pallas_call(
        functools.partial(compute, sizes),
        out_shape=[jax.ShapeDtypeStruct(flat[i].shape, f32) for i in (0, 1, 2, 3, 1)],
        in_specs=[smem] * 2 + [vmem] * (7 + 1 + 6 * sides),
        out_specs=[vmem] * 5,
        scratch_shapes=[
            pltpu.VMEM((2 * rows, cols), f32),
            pltpu.VMEM((rows + 6, state, span), f32),
            pltpu.VMEM((rows + 4, fields, span), f32),
            pltpu.VMEM((rows + 2, fields, span), f32),
            pltpu.VMEM((rows + 6, layers, span), f32),
            pltpu.VMEM((rows + 6, layers, span), f32),
            pltpu.VMEM((5, rows + 2, layers, span), f32),
            pltpu.VMEM((rows + 2, layers, span), f32),
            pltpu.VMEM((rows + 2, layers, span), f32),
        ],
        compiler_params=pltpu.CompilerParams(vmem_limit_bytes=32 * 1024 * 1024),
        name="ocean_step",
    )(row_biome, growth_rates, *flat, land_mask, bottom_layer, reaction_rates, *got)
    return (
        outs[0].reshape(velocity.shape),
        outs[1].reshape(thickness.shape),
        outs[2].reshape(hydrography.shape),
        outs[3].reshape(tracers.shape),
        outs[4].reshape(thickness.shape),
    )


def solution(mesh):
    in_specs = (
        P(None, None, "lat", "lon"),
        P(None, "lat", "lon"),
        P(None, None, "lat", "lon"),
        P(None, None, "lat", "lon"),
        P("lat", "lon"),
        P("lat", "lon"),
        P("lat"),
        P(),
        P(),
    )
    out_specs = (
        P(None, None, "lat", "lon"),
        P(None, "lat", "lon"),
        P(None, None, "lat", "lon"),
        P(None, None, "lat", "lon"),
        P(None, "lat", "lon"),
    )
    return jax.shard_map(
        per_device, mesh=mesh, in_specs=in_specs, out_specs=out_specs, check_vma=False
    )
```

```python
import functools

import jax
import jax.numpy as jnp
from jax import lax
from jax.experimental import pallas as pl
from jax.experimental.pallas import tpu as pltpu
from jax.sharding import PartitionSpec as P

NSUB = 2
heat_coef = 0.2
salt_coef = 0.25
gravity = 0.3
viscosity = 0.1
coriolis_coef = 0.3
tracer_diff = 0.1
kappa_base = 0.02
kappa_var = 0.1
water_att = 0.1
chlorophyll_att = 0.2
heat_gain = 1.0
MESH = pl.DeviceIdType.MESH


def growth_of(biome, growth, row, kinds):
    value = jnp.float32(0.0)
    for kind in range(kinds):
        value = jnp.where(biome[row] == kind, growth[kind], value)
    return value


def write_misc(misc, land, bottom, biome, growth, rows, cols, kinds):
    misc[0:rows, :] = (land[...] * bottom[...]).astype(jnp.float32)
    for row in range(rows):
        misc[rows + row : rows + row + 1, :] = jnp.full(
            (1, cols), growth_of(biome, growth, row, kinds), jnp.float32
        )


def exchange(sizes, biome, growth, *refs):
    held, refs = refs[:6], refs[6:]
    lats, lons, layers, rows, cols, kinds, near, sides = sizes
    fields = held[3].shape[0] // rows
    got_ns = refs[0]
    got_lon = [refs[1 + 6 * i : 7 + 6 * i] for i in range(sides)]
    misc, pack, send_ns, recv_ns, send_lon, recv_lon, load_sem = refs[1 + 6 * sides : 8 + 6 * sides]
    local = refs[8 + 6 * sides :]
    vel, thick, hydro, tracers, land, bottom = local
    loads = [
        pltpu.make_async_copy(held[i], local[i], load_sem.at[i]) for i in (4, 5, 3, 0, 2, 1)
    ]
    for load in loads:
        load.start()
    lat, lon = lax.axis_index("lat"), lax.axis_index("lon")
    barrier = pltpu.get_barrier_semaphore()
    around = [
        (lat > 0, (lat - 1, lon)),
        (lat < lats - 1, (lat + 1, lon)),
        (lon > 0, (lat, lon - 1)),
        (lon < lons - 1, (lat, lon + 1)),
    ]
    for there, where in around:

        @pl.when(there)
        def _(where=where):
            pl.semaphore_signal(barrier, inc=1, device_id=where, device_id_type=MESH)

    for load in loads[:2]:
        load.wait()
    write_misc(misc, land, bottom, biome, growth, rows, cols, kinds)
    for load in loads[2:]:
        load.wait()

    def state_row(side, start, row):
        for ref, count in ((vel, 2 * layers), (thick, layers), (hydro, 2 * layers)):
            pack[side, start : start + count, :] = ref[pl.ds(row, count, stride=rows), :]
            start += count

    def second_row(side, start, row):
        flow, one = 2 * layers, layers
        pack[side, start : start + flow, :] = vel[pl.ds(row, flow, stride=rows), :]
        pack[side, start + flow : start + flow + one, :] = thick[pl.ds(row, one, stride=rows), :]
        warm = hydro[pl.ds(row, one, stride=rows), :]
        salt = hydro[pl.ds(one * rows + row, one, stride=rows), :]
        pack[side, start + flow + one : start + flow + 2 * one, :] = (
            salt_coef * salt - heat_coef * warm
        )

    def third_row(side, start, row):
        one = layers
        pack[side, start : start + one, :] = vel[pl.ds(one * rows + row, one, stride=rows), :]
        pack[side, start + one : start + 2 * one, :] = thick[pl.ds(row, one, stride=rows), :]

    def tracer_row(side, start, row):
        pack[side, start : start + fields, :] = tracers[pl.ds(row, fields, stride=rows), :]

    state = 5 * layers
    for side in range(2):
        order = (rows - 1, rows - 2, rows - 3) if side == 0 else (0, 1, 2)
        state_row(side, 0, order[0])
        tracer_row(side, state, order[0])
        second_row(side, state + fields, order[1])
        pack[side, near - 2 * rows : near, :] = misc[...]
        tracer_row(side, near, order[1])
        third_row(side, near + fields, order[2])

    peers = sum(there.astype(jnp.int32) for there, _ in around)
    pl.semaphore_wait(barrier, peers)

    def ns_copy(side, part):
        to = lat + 1 if side == 0 else lat - 1
        return pltpu.make_async_remote_copy(
            src_ref=pack.at[side, cuts[part] : cuts[part + 1]],
            dst_ref=got_ns.at[side, cuts[part] : cuts[part + 1]],
            send_sem=send_ns.at[side, part],
            recv_sem=recv_ns.at[side, part],
            device_id=(to, lon),
            device_id_type=MESH,
        )

    def lon_copy(way, item):
        slot = way if sides == 2 else 0
        to = lon + 1 if way == 0 else lon - 1
        if item < 5:
            src = (*held[:4], misc)[item]
            dst = got_lon[slot][item]
        else:
            src = got_ns.at[item - 5, 0:near]
            dst = got_lon[slot][5].at[item - 5]
        return pltpu.make_async_remote_copy(
            src_ref=src,
            dst_ref=dst,
            send_sem=send_lon.at[way, item],
            recv_sem=recv_lon.at[way, item],
            device_id=(lat, to),
            device_id_type=MESH,
        )

    cuts = (0, near, got_ns.shape[1])
    south, north = lat > 0, lat < lats - 1
    west, east = lon > 0, lon < lons - 1
    ns_send = (north, south)
    ns_recv = (south, north)
    lon_send = (east, west)
    lon_recv = (west, east)
    for part in range(2):
        for side in range(2):

            @pl.when(ns_send[side])
            def _(side=side, part=part):
                ns_copy(side, part).start()

    for way in range(2):

        @pl.when(lon_send[way])
        def _(way=way):
            for item in range(5):
                lon_copy(way, item).start()

    for side in range(2):

        @pl.when(ns_recv[side])
        def _(side=side):
            ns_copy(side, 0).wait_recv()
            for way in range(2):

                @pl.when(lon_send[way])
                def _(way=way):
                    lon_copy(way, 5 + side).start()

    for way in range(2):

        @pl.when(lon_recv[way])
        def _(way=way):
            for item in range(5):
                lon_copy(way, item).wait_recv()
            for side in range(2):

                @pl.when(ns_recv[side])
                def _(side=side):
                    lon_copy(way, 5 + side).wait_recv()

        @pl.when(lon_send[way])
        def _(way=way):
            for item in range(5):
                lon_copy(way, item).wait_send()
            for side in range(2):

                @pl.when(ns_recv[side])
                def _(side=side):
                    lon_copy(way, 5 + side).wait_send()

    for side in range(2):

        @pl.when(ns_recv[side])
        def _(side=side):
            ns_copy(side, 1).wait_recv()

        @pl.when(ns_send[side])
        def _(side=side):
            ns_copy(side, 0).wait_send()
            ns_copy(side, 1).wait_send()


def to_east(values):
    return pltpu.roll(values, values.shape[-1] - 1, values.ndim - 1)


def to_west(values):
    return pltpu.roll(values, 1, values.ndim - 1)


def load_all(body, count, biome, growth, *refs):
    held, outs = refs[:count], refs[count : count + 5]
    local, rest, sems = refs[count + 5 : 2 * count + 5], refs[2 * count + 5 : -1], refs[-1]
    loads = [pltpu.make_async_copy(held[i], local[i], sems.at[i]) for i in range(count)]
    for load in loads:
        load.start()
    for load in loads:
        load.wait()
    body(biome, growth, *local, *outs, *rest)


def compute(sizes, biome, growth, vel, thick, hydro, tracers, land, bottom, rates, *refs):
    lats, lons, layers, rows, cols, kinds, near, sides = sizes
    fields = tracers.shape[0] // rows
    ntr = fields // layers
    got_ns = refs[0]
    got_lon = [refs[1 + 6 * i : 7 + 6 * i] for i in range(sides)]
    out_vel, out_thick, out_hydro, out_tr, out_abs = refs[1 + 6 * sides : 6 + 6 * sides]
    misc, st, tr, mid, depth, grow, coef, glow, wets = refs[6 + 6 * sides :]
    lat, lon = lax.axis_index("lat"), lax.axis_index("lon")
    span = 2 * cols
    state = 5 * layers
    write_misc(misc, land, bottom, biome, growth, rows, cols, kinds)

    lanes = lax.broadcasted_iota(jnp.int32, (1, cols), 1)
    first = lanes < cols // 2
    lane_e = jnp.logical_and(first, lon < lons - 1)
    lane_w = jnp.logical_and(jnp.logical_not(first), lon > 0)

    def beside(load, mask=None):
        west_part = load(got_lon[0])
        east_part = load(got_lon[-1])
        use_e, use_w = lane_e, lane_w
        if mask is not None:
            use_e, use_w = jnp.logical_and(use_e, mask), jnp.logical_and(use_w, mask)
        return jnp.where(use_e, east_part, jnp.where(use_w, west_part, 0.0))

    def both(ref, at, start, own, side_values):
        count = own.shape[0]
        ref[at, start : start + count, 0:cols] = own
        ref[at, start : start + count, cols:span] = side_values

    for row in range(rows):
        start = 0
        for item, (ref, count) in enumerate(
            ((vel, 2 * layers), (thick, layers), (hydro, 2 * layers))
        ):
            pick = pl.ds(row, count, stride=rows)
            both(
                st, 3 + row, start, ref[pick, :], beside(lambda got, i=item, p=pick: got[i][p, :])
            )
            start += count
        pick = pl.ds(row, fields, stride=rows)
        both(tr, 2 + row, 0, tracers[pick, :], beside(lambda got, p=pick: got[3][p, :]))
    for ref, begin in ((depth, 0), (grow, rows)):
        for row in range(rows):
            pick = slice(begin + row, begin + row + 1)
            ref[3 + row, :, 0:cols] = jnp.broadcast_to(misc[pick, :], (layers, cols))
            ref[3 + row, :, cols:span] = jnp.broadcast_to(
                beside(lambda got, p=pick: got[4][p, :]), (layers, cols)
            )
    for side in range(2):
        there = lat > 0 if side == 0 else lat < lats - 1
        mask = jnp.logical_and(lanes >= 0, there)

        def own_part(begin, count, side=side, mask=mask):
            return jnp.where(mask, got_ns[side, begin : begin + count, :], 0.0)

        def far_part(begin, count, side=side, mask=mask):
            return beside(lambda got: got[5][side, begin : begin + count, :], mask)

        place = (2, 1, 0) if side == 0 else (rows + 3, rows + 4, rows + 5)
        place_tr = (1, 0) if side == 0 else (rows + 2, rows + 3)
        source = (rows - 1, rows - 2, rows - 3) if side == 0 else (0, 1, 2)
        both(st, place[0], 0, own_part(0, state), far_part(0, state))
        both(tr, place_tr[0], 0, own_part(state, fields), far_part(state, fields))
        both(
            st,
            place[1],
            0,
            own_part(state + fields, 3 * layers),
            far_part(state + fields, 3 * layers),
        )
        empty = jnp.zeros((layers, cols), jnp.float32)
        at = state + fields + 3 * layers
        both(st, place[1], 3 * layers, empty, empty)
        scale = 1.0 / salt_coef
        both(
            st, place[1], 4 * layers, scale * own_part(at, layers), scale * far_part(at, layers)
        )
        both(tr, place_tr[1], 0, own_part(near, fields), jnp.zeros((fields, cols), jnp.float32))
        nothing = jnp.zeros((state, cols), jnp.float32)
        both(st, place[2], 0, nothing, nothing)
        st[place[2], layers : 3 * layers, 0:cols] = own_part(near + fields, 2 * layers)
        begin = near - 2 * rows
        for ref, extra in ((depth, 0), (grow, rows)):
            for step in range(3):
                at = begin + extra + source[step]
                ref[place[step], :, 0:cols] = jnp.broadcast_to(own_part(at, 1), (layers, cols))
                ref[place[step], :, cols:span] = jnp.broadcast_to(far_part(at, 1), (layers, cols))

    total = rows * lats
    deep = rows + 6
    base = (lat * rows).astype(jnp.float32)

    def latitude(begin, count):
        at = lax.broadcasted_iota(jnp.int32, (count, layers, span), 0).astype(jnp.float32)
        return 2.0 * ((base + (at + begin)) + 0.5) / total - 1.0

    level = lax.broadcasted_iota(jnp.int32, (1, layers, span), 1)
    wet = (level.astype(jnp.float32) < depth[...]).astype(jnp.float32)
    wet_e = wet * to_east(wet)
    wet_n = wet[:-1] * wet[1:]
    u = st[:, 0:layers, :]
    v = st[:, layers : 2 * layers, :]
    h = st[:, 2 * layers : 3 * layers, :]
    warm = st[:, 3 * layers : 4 * layers, :]
    salt = st[:, 4 * layers : 5 * layers, :]

    def inner(a):
        return a[1 : deep - 1]

    def laplace(a, low, high):
        block, eface = a[low:high], wet_e[low:high]
        fe = eface * (to_east(block) - block)
        fn = wet_n[low - 1 : high] * (a[low : high + 1] - a[low - 1 : high])
        return fe - to_west(fe) + fn[1:] - fn[:-1]

    dens = salt_coef * salt - heat_coef * warm
    press = gravity * h + dens
    cor = coriolis_coef * latitude(-2.0, deep - 2)
    new_u = inner(wet_e) * (
        inner(u)
        + cor * inner(v)
        - (to_east(inner(press)) - inner(press))
        + viscosity * laplace(u, 1, deep - 1)
    )
    new_v = wet_n[1:] * (
        inner(v)
        - cor * inner(u)
        - (press[2:] - inner(press))
        + viscosity * laplace(v, 1, deep - 1)
    )
    q_e = inner(wet_e * u * 0.5 * (h + to_east(h)))
    q_n = wet_n * v[:-1] * 0.5 * (h[:-1] + h[1:])
    new_h = inner(wet) * (inner(h) - (q_e - to_west(q_e) + q_n[1:] - q_n[:-1]))
    dens = inner(dens)
    below = jnp.where(level < layers - 1, pltpu.roll(dens, layers - 1, 1) - dens, 0.0)
    kappa = inner(wet) * (kappa_base + kappa_var / (1.0 + 10.0 * below * below))

    def upwind(flow, spread):
        return jnp.maximum(flow, 0.0) + spread, jnp.minimum(flow, 0.0) - spread

    he, ke = new_h[1:-1], kappa[1:-1]
    face_e, face_n = wet_e[2:-2], wet_n[1:-1]
    a_e, b_e = upwind(
        face_e * new_u[1:-1] * 0.5 * (he + to_east(he)), face_e * 0.5 * (ke + to_east(ke))
    )
    a_n, b_n = upwind(
        face_n * new_v[:-1] * 0.5 * (new_h[:-1] + new_h[1:]),
        face_n * 0.5 * (kappa[:-1] + kappa[1:]),
    )
    sub = 1.0 / NSUB
    a_w, b_w = to_west(a_e), to_west(b_e)
    coef[0] = 1.0 - sub * (a_e - b_w + a_n[1:] - b_n[:-1])
    coef[1] = -sub * b_e
    coef[2] = sub * a_w
    coef[3] = -sub * b_n[1:]
    coef[4] = sub * a_n[:-1]
    wet_in = wet[2:-2]
    wets[...] = wet_in

    chl = tr[1 : rows + 3, layers : 2 * layers, :]
    att = wet_in * (water_att + chlorophyll_att * chl * chl)
    summed = att
    step = 1
    while step < layers:
        summed = summed + jnp.where(level >= step, pltpu.roll(summed, step, 1), 0.0)
        step *= 2
    lat_in = latitude(-1.0, rows + 2)
    top = (1.0 - 0.8 * lat_in * lat_in) * jnp.exp(att - summed)
    glow[...] = grow[2 : rows + 4] * top
    light = (top * (1.0 - jnp.exp(-att)))[1:-1, :, 0:cols]
    mine = wet[3:-3, :, 0:cols]
    mixed_t = (
        mine * (warm[3:-3] + tracer_diff * laplace(warm, 3, deep - 3))[:, :, 0:cols]
        + heat_gain * light
    )
    mixed_s = mine * (salt[3:-3] + tracer_diff * laplace(salt, 3, deep - 3))[:, :, 0:cols]
    for row in range(rows):
        pick = pl.ds(row, layers, stride=rows)
        later = pl.ds(layers * rows + row, layers, stride=rows)
        out_vel[pick, :] = new_u[2 + row, :, 0:cols]
        out_vel[later, :] = new_v[2 + row, :, 0:cols]
        out_thick[pick, :] = new_h[2 + row, :, 0:cols]
        out_hydro[pick, :] = mixed_t[row]
        out_hydro[later, :] = mixed_s[row]
        out_abs[pick, :] = light[row]

    wide = lax.broadcasted_iota(jnp.int32, (fields, ntr), 0) // layers
    pick_t = (wide == lax.broadcasted_iota(jnp.int32, (fields, ntr), 1)).astype(jnp.float32)
    spread_rates = jnp.dot(
        pick_t,
        lax.dot_general(
            rates[...],
            pick_t,
            (((1,), (1,)), ((), ())),
            precision=lax.Precision.HIGHEST,
            preferred_element_type=jnp.float32,
        ),
        precision=lax.Precision.HIGHEST,
        preferred_element_type=jnp.float32,
    )
    same = (
        lax.broadcasted_iota(jnp.int32, (fields, fields), 0) % layers
        == lax.broadcasted_iota(jnp.int32, (fields, fields), 1) % layers
    )
    couple = jnp.where(same, sub * spread_rates, 0.0)
    couple_hi = couple.astype(jnp.bfloat16)
    couple_lo = (couple - couple_hi.astype(jnp.float32)).astype(jnp.bfloat16)

    def advance(src, at, width):
        c = src[at + 1].reshape(ntr, layers, span)
        up = src[at + 2].reshape(ntr, layers, span)[:, :, 0:width]
        down = src[at].reshape(ntr, layers, span)[:, :, 0:width]
        return c, up, down

    def finish(src, at, face, width):
        c, up, down = advance(src, at, width)
        k = [coef[i, face, :, 0:width] for i in range(5)]
        adv = (
            k[0] * c[:, :, 0:width]
            + k[1] * to_east(c)[:, :, 0:width]
            + k[2] * to_west(c)[:, :, 0:width]
            + k[3] * up
            + k[4] * down
        )
        flat = adv.reshape(fields, width)
        hi = flat.astype(jnp.bfloat16)
        lo = (flat - hi.astype(jnp.float32)).astype(jnp.bfloat16)

        def mul(a, b):
            return jnp.dot(a, b, preferred_element_type=jnp.float32)

        new = flat + (mul(couple_hi, hi) + (mul(couple_hi, lo) + mul(couple_lo, hi)))
        nut, plk = adv[0], adv[1]
        uptake = glow[face, :, 0:width] * plk * nut * nut / (1.0 + nut * nut)
        new = new.reshape(ntr, layers, width)
        w = wets[face, :, 0:width]
        first_two = (
            w * (new[0] - sub * uptake),
            w * (new[1] + sub * uptake),
        )
        return (w * new).reshape(fields, width), first_two

    def first_step(at, carry):
        new, (zero, one) = finish(tr, at, at, span)
        mid[at] = new
        mid[at, 0:layers, :] = zero
        mid[at, layers : 2 * layers, :] = one
        return carry

    lax.fori_loop(0, rows + 2, first_step, 0)
    for row in range(rows):
        new, (zero, one) = finish(mid, row, row + 1, cols)
        out_tr[pl.ds(row, fields, stride=rows), :] = new
        out_tr[pl.ds(row, layers, stride=rows), :] = zero
        out_tr[pl.ds(layers * rows + row, layers, stride=rows), :] = one


def per_device(
    velocity,
    thickness,
    hydrography,
    tracers,
    land_mask,
    bottom_layer,
    row_biome,
    reaction_rates,
    growth_rates,
):
    ntr, layers, rows, cols = tracers.shape
    lats, lons = lax.axis_size("lat"), lax.axis_size("lon")
    state, fields = 5 * layers, ntr * layers
    near = state + fields + 4 * layers + 2 * rows
    whole = near + fields + 2 * layers
    sides = 1 if lons <= 2 else 2
    sizes = (lats, lons, layers, rows, cols, growth_rates.shape[0], near, sides)
    flat = [a.reshape(-1, cols) for a in (velocity, thickness, hydrography, tracers)]
    vmem = pl.BlockSpec(memory_space=pltpu.VMEM)
    smem = pl.BlockSpec(memory_space=pltpu.SMEM)
    hbm = pl.BlockSpec(memory_space=pltpu.HBM)
    f32 = jnp.float32
    lon_shapes = [jax.ShapeDtypeStruct(a.shape, f32) for a in flat] + [
        jax.ShapeDtypeStruct((2 * rows, cols), f32),
        jax.ShapeDtypeStruct((2, near, cols), f32),
    ]
    got = pl.pallas_call(
        functools.partial(exchange, sizes),
        out_shape=[jax.ShapeDtypeStruct((2, whole, cols), f32)] + lon_shapes * sides,
        in_specs=[smem] * 2 + [hbm] * 6,
        out_specs=[pl.BlockSpec(memory_space=pl.ANY)] * (1 + 6 * sides),
        scratch_shapes=[
            pltpu.VMEM((2 * rows, cols), f32),
            pltpu.VMEM((2, whole, cols), f32),
            pltpu.SemaphoreType.DMA((2, 2)),
            pltpu.SemaphoreType.DMA((2, 2)),
            pltpu.SemaphoreType.DMA((2, 7)),
            pltpu.SemaphoreType.DMA((2, 7)),
            pltpu.SemaphoreType.DMA((6,)),
            *[pltpu.VMEM(a.shape, f32) for a in flat],
            pltpu.VMEM((rows, cols), jnp.int32),
            pltpu.VMEM((rows, cols), jnp.int32),
        ],
        compiler_params=pltpu.CompilerParams(
            collective_id=0, has_side_effects=True, vmem_limit_bytes=62 * 1024 * 1024
        ),
        name="exchange",
    )(row_biome, growth_rates, *flat, land_mask, bottom_layer)
    span = 2 * cols
    operands = [*flat, land_mask, bottom_layer, reaction_rates, *got]
    count = len(operands)
    outs = pl.pallas_call(
        functools.partial(load_all, functools.partial(compute, sizes), count),
        out_shape=[jax.ShapeDtypeStruct(flat[i].shape, f32) for i in (0, 1, 2, 3, 1)],
        in_specs=[smem] * 2 + [hbm] * count,
        out_specs=[vmem] * 5,
        scratch_shapes=[pltpu.VMEM(a.shape, a.dtype) for a in operands]
        + [
            pltpu.VMEM((2 * rows, cols), f32),
            pltpu.VMEM((rows + 6, state, span), f32),
            pltpu.VMEM((rows + 4, fields, span), f32),
            pltpu.VMEM((rows + 2, fields, span), f32),
            pltpu.VMEM((rows + 6, layers, span), f32),
            pltpu.VMEM((rows + 6, layers, span), f32),
            pltpu.VMEM((5, rows + 2, layers, span), f32),
            pltpu.VMEM((rows + 2, layers, span), f32),
            pltpu.VMEM((rows + 2, layers, span), f32),
            pltpu.SemaphoreType.DMA((count,)),
        ],
        compiler_params=pltpu.CompilerParams(vmem_limit_bytes=62 * 1024 * 1024),
        name="ocean_step",
    )(row_biome, growth_rates, *operands)
    return (
        outs[0].reshape(velocity.shape),
        outs[1].reshape(thickness.shape),
        outs[2].reshape(hydrography.shape),
        outs[3].reshape(tracers.shape),
        outs[4].reshape(thickness.shape),
    )


def solution(mesh):
    in_specs = (
        P(None, None, "lat", "lon"),
        P(None, "lat", "lon"),
        P(None, None, "lat", "lon"),
        P(None, None, "lat", "lon"),
        P("lat", "lon"),
        P("lat", "lon"),
        P("lat"),
        P(),
        P(),
    )
    out_specs = (
        P(None, None, "lat", "lon"),
        P(None, "lat", "lon"),
        P(None, None, "lat", "lon"),
        P(None, None, "lat", "lon"),
        P(None, "lat", "lon"),
    )
    return jax.shard_map(
        per_device, mesh=mesh, in_specs=in_specs, out_specs=out_specs, check_vma=False
    )
```

```python
import functools

import jax
import jax.numpy as jnp
from jax import lax
from jax.experimental import pallas as pl
from jax.experimental.pallas import tpu as pltpu
from jax.sharding import PartitionSpec as P

NSUB = 2
heat_coef = 0.2
salt_coef = 0.25
gravity = 0.3
viscosity = 0.1
coriolis_coef = 0.3
tracer_diff = 0.1
kappa_base = 0.02
kappa_var = 0.1
water_att = 0.1
chlorophyll_att = 0.2
heat_gain = 1.0
MESH = pl.DeviceIdType.MESH


def growth_of(biome, growth, row, kinds):
    value = jnp.float32(0.0)
    for kind in range(kinds):
        value = jnp.where(biome[row] == kind, growth[kind], value)
    return value


def write_misc(misc, land, bottom, biome, growth, rows, cols, kinds):
    misc[0:rows, :] = (land[...] * bottom[...]).astype(jnp.float32)
    for row in range(rows):
        misc[rows + row : rows + row + 1, :] = jnp.full(
            (1, cols), growth_of(biome, growth, row, kinds), jnp.float32
        )


def exchange(sizes, biome, growth, *refs):
    held, refs = refs[:6], refs[6:]
    lats, lons, layers, rows, cols, kinds, near, sides = sizes
    fields = held[3].shape[0] // rows
    got_ns = refs[0]
    got_lon = [refs[1 + 6 * i : 7 + 6 * i] for i in range(sides)]
    misc, pack, send_ns, recv_ns, send_lon, recv_lon, load_sem = refs[1 + 6 * sides : 8 + 6 * sides]
    local = refs[8 + 6 * sides :]
    vel, thick, hydro, tracers, land, bottom = local
    loads = [
        pltpu.make_async_copy(held[i], local[i], load_sem.at[i]) for i in (4, 5, 3, 0, 2, 1)
    ]
    for load in loads:
        load.start()
    lat, lon = lax.axis_index("lat"), lax.axis_index("lon")
    barrier = pltpu.get_barrier_semaphore()
    around = [
        (lat > 0, (lat - 1, lon)),
        (lat < lats - 1, (lat + 1, lon)),
        (lon > 0, (lat, lon - 1)),
        (lon < lons - 1, (lat, lon + 1)),
    ]
    for there, where in around:

        @pl.when(there)
        def _(where=where):
            pl.semaphore_signal(barrier, inc=1, device_id=where, device_id_type=MESH)

    for load in loads[:2]:
        load.wait()
    write_misc(misc, land, bottom, biome, growth, rows, cols, kinds)
    for load in loads[2:]:
        load.wait()

    def state_row(side, start, row):
        for ref, count in ((vel, 2 * layers), (thick, layers), (hydro, 2 * layers)):
            pack[side, start : start + count, :] = ref[pl.ds(row, count, stride=rows), :]
            start += count

    def second_row(side, start, row):
        flow, one = 2 * layers, layers
        pack[side, start : start + flow, :] = vel[pl.ds(row, flow, stride=rows), :]
        pack[side, start + flow : start + flow + one, :] = thick[pl.ds(row, one, stride=rows), :]
        warm = hydro[pl.ds(row, one, stride=rows), :]
        salt = hydro[pl.ds(one * rows + row, one, stride=rows), :]
        pack[side, start + flow + one : start + flow + 2 * one, :] = (
            salt_coef * salt - heat_coef * warm
        )

    def third_row(side, start, row):
        one = layers
        pack[side, start : start + one, :] = vel[pl.ds(one * rows + row, one, stride=rows), :]
        pack[side, start + one : start + 2 * one, :] = thick[pl.ds(row, one, stride=rows), :]

    def tracer_row(side, start, row):
        pack[side, start : start + fields, :] = tracers[pl.ds(row, fields, stride=rows), :]

    state = 5 * layers
    for side in range(2):
        order = (rows - 1, rows - 2, rows - 3) if side == 0 else (0, 1, 2)
        state_row(side, 0, order[0])
        tracer_row(side, state, order[0])
        second_row(side, state + fields, order[1])
        pack[side, near - 2 * rows : near, :] = misc[...]
        tracer_row(side, near, order[1])
        third_row(side, near + fields, order[2])

    peers = sum(there.astype(jnp.int32) for there, _ in around)
    pl.semaphore_wait(barrier, peers)

    def ns_copy(side, part):
        to = lat + 1 if side == 0 else lat - 1
        return pltpu.make_async_remote_copy(
            src_ref=pack.at[side, cuts[part] : cuts[part + 1]],
            dst_ref=got_ns.at[side, cuts[part] : cuts[part + 1]],
            send_sem=send_ns.at[side, part],
            recv_sem=recv_ns.at[side, part],
            device_id=(to, lon),
            device_id_type=MESH,
        )

    def lon_copy(way, item):
        slot = way if sides == 2 else 0
        to = lon + 1 if way == 0 else lon - 1
        if item < 5:
            src = (*held[:4], misc)[item]
            dst = got_lon[slot][item]
        else:
            src = got_ns.at[item - 5, 0:near]
            dst = got_lon[slot][5].at[item - 5]
        return pltpu.make_async_remote_copy(
            src_ref=src,
            dst_ref=dst,
            send_sem=send_lon.at[way, item],
            recv_sem=recv_lon.at[way, item],
            device_id=(lat, to),
            device_id_type=MESH,
        )

    cuts = (0, near, got_ns.shape[1])
    south, north = lat > 0, lat < lats - 1
    west, east = lon > 0, lon < lons - 1
    ns_send = (north, south)
    ns_recv = (south, north)
    lon_send = (east, west)
    lon_recv = (west, east)
    for part in range(2):
        for side in range(2):

            @pl.when(ns_send[side])
            def _(side=side, part=part):
                ns_copy(side, part).start()

    for way in range(2):

        @pl.when(lon_send[way])
        def _(way=way):
            for item in range(5):
                lon_copy(way, item).start()

    for side in range(2):

        @pl.when(ns_recv[side])
        def _(side=side):
            ns_copy(side, 0).wait_recv()
            for way in range(2):

                @pl.when(lon_send[way])
                def _(way=way):
                    lon_copy(way, 5 + side).start()

    for way in range(2):

        @pl.when(lon_recv[way])
        def _(way=way):
            for item in range(5):
                lon_copy(way, item).wait_recv()
            for side in range(2):

                @pl.when(ns_recv[side])
                def _(side=side):
                    lon_copy(way, 5 + side).wait_recv()

        @pl.when(lon_send[way])
        def _(way=way):
            for item in range(5):
                lon_copy(way, item).wait_send()
            for side in range(2):

                @pl.when(ns_recv[side])
                def _(side=side):
                    lon_copy(way, 5 + side).wait_send()

    for side in range(2):

        @pl.when(ns_recv[side])
        def _(side=side):
            ns_copy(side, 1).wait_recv()

        @pl.when(ns_send[side])
        def _(side=side):
            ns_copy(side, 0).wait_send()
            ns_copy(side, 1).wait_send()


def to_east(values):
    return pltpu.roll(values, values.shape[-1] - 1, values.ndim - 1)


def to_west(values):
    return pltpu.roll(values, 1, values.ndim - 1)


def load_all(body, count, biome, growth, *refs):
    held, outs = refs[:count], refs[count : count + 5]
    local, rest, sems = refs[count + 5 : 2 * count + 5], refs[2 * count + 5 : -1], refs[-1]
    loads = [pltpu.make_async_copy(held[i], local[i], sems.at[i]) for i in range(count)]
    for load in loads:
        load.start()
    body(loads, biome, growth, *local, *outs, *rest)


def compute(sizes, loads, biome, growth, vel, thick, hydro, tracers, land, bottom, rates, *refs):
    lats, lons, layers, rows, cols, kinds, near, sides = sizes
    fields = tracers.shape[0] // rows
    ntr = fields // layers
    got_ns = refs[0]
    got_lon = [refs[1 + 6 * i : 7 + 6 * i] for i in range(sides)]
    out_vel, out_thick, out_hydro, out_tr, out_abs = refs[1 + 6 * sides : 6 + 6 * sides]
    misc, st, tr, mid, depth, grow, coef, glow, wets = refs[6 + 6 * sides :]
    lat, lon = lax.axis_index("lat"), lax.axis_index("lon")
    span = 2 * cols
    state = 5 * layers
    for load in loads[:7]:
        load.wait()
    write_misc(misc, land, bottom, biome, growth, rows, cols, kinds)
    for row in range(rows):
        start = 0
        for ref, count in ((vel, 2 * layers), (thick, layers), (hydro, 2 * layers)):
            st[3 + row, start : start + count, 0:cols] = ref[pl.ds(row, count, stride=rows), :]
            start += count
        tr[2 + row, :, 0:cols] = tracers[pl.ds(row, fields, stride=rows), :]

    lanes = lax.broadcasted_iota(jnp.int32, (1, cols), 1)
    first = lanes < cols // 2
    lane_e = jnp.logical_and(first, lon < lons - 1)
    lane_w = jnp.logical_and(jnp.logical_not(first), lon > 0)

    def beside(load, mask=None):
        west_part = load(got_lon[0])
        east_part = load(got_lon[-1])
        use_e, use_w = lane_e, lane_w
        if mask is not None:
            use_e, use_w = jnp.logical_and(use_e, mask), jnp.logical_and(use_w, mask)
        return jnp.where(use_e, east_part, jnp.where(use_w, west_part, 0.0))

    def both(ref, at, start, own, side_values):
        count = own.shape[0]
        ref[at, start : start + count, 0:cols] = own
        ref[at, start : start + count, cols:span] = side_values

    wide = lax.broadcasted_iota(jnp.int32, (fields, ntr), 0) // layers
    pick_t = (wide == lax.broadcasted_iota(jnp.int32, (fields, ntr), 1)).astype(jnp.float32)
    spread_rates = jnp.dot(
        pick_t,
        lax.dot_general(
            rates[...],
            pick_t,
            (((1,), (1,)), ((), ())),
            precision=lax.Precision.HIGHEST,
            preferred_element_type=jnp.float32,
        ),
        precision=lax.Precision.HIGHEST,
        preferred_element_type=jnp.float32,
    )
    same = (
        lax.broadcasted_iota(jnp.int32, (fields, fields), 0) % layers
        == lax.broadcasted_iota(jnp.int32, (fields, fields), 1) % layers
    )
    couple = jnp.where(same, spread_rates / NSUB, 0.0)
    couple_hi = couple.astype(jnp.bfloat16)
    couple_lo = (couple - couple_hi.astype(jnp.float32)).astype(jnp.bfloat16)

    for load in loads[7:]:
        load.wait()
    for row in range(rows):
        start = 0
        for item, count in enumerate((2 * layers, layers, 2 * layers)):
            pick = pl.ds(row, count, stride=rows)
            st[3 + row, start : start + count, cols:span] = beside(
                lambda got, i=item, p=pick: got[i][p, :]
            )
            start += count
        pick = pl.ds(row, fields, stride=rows)
        tr[2 + row, :, cols:span] = beside(lambda got, p=pick: got[3][p, :])
    for ref, begin in ((depth, 0), (grow, rows)):
        for row in range(rows):
            pick = slice(begin + row, begin + row + 1)
            ref[3 + row, :, 0:cols] = jnp.broadcast_to(misc[pick, :], (layers, cols))
            ref[3 + row, :, cols:span] = jnp.broadcast_to(
                beside(lambda got, p=pick: got[4][p, :]), (layers, cols)
            )
    for side in range(2):
        there = lat > 0 if side == 0 else lat < lats - 1
        mask = jnp.logical_and(lanes >= 0, there)

        def own_part(begin, count, side=side, mask=mask):
            return jnp.where(mask, got_ns[side, begin : begin + count, :], 0.0)

        def far_part(begin, count, side=side, mask=mask):
            return beside(lambda got: got[5][side, begin : begin + count, :], mask)

        place = (2, 1, 0) if side == 0 else (rows + 3, rows + 4, rows + 5)
        place_tr = (1, 0) if side == 0 else (rows + 2, rows + 3)
        source = (rows - 1, rows - 2, rows - 3) if side == 0 else (0, 1, 2)
        both(st, place[0], 0, own_part(0, state), far_part(0, state))
        both(tr, place_tr[0], 0, own_part(state, fields), far_part(state, fields))
        both(
            st,
            place[1],
            0,
            own_part(state + fields, 3 * layers),
            far_part(state + fields, 3 * layers),
        )
        empty = jnp.zeros((layers, cols), jnp.float32)
        at = state + fields + 3 * layers
        both(st, place[1], 3 * layers, empty, empty)
        scale = 1.0 / salt_coef
        both(
            st, place[1], 4 * layers, scale * own_part(at, layers), scale * far_part(at, layers)
        )
        both(tr, place_tr[1], 0, own_part(near, fields), jnp.zeros((fields, cols), jnp.float32))
        nothing = jnp.zeros((state, cols), jnp.float32)
        both(st, place[2], 0, nothing, nothing)
        st[place[2], layers : 3 * layers, 0:cols] = own_part(near + fields, 2 * layers)
        begin = near - 2 * rows
        for ref, extra in ((depth, 0), (grow, rows)):
            for step in range(3):
                at = begin + extra + source[step]
                ref[place[step], :, 0:cols] = jnp.broadcast_to(own_part(at, 1), (layers, cols))
                ref[place[step], :, cols:span] = jnp.broadcast_to(far_part(at, 1), (layers, cols))

    total = rows * lats
    deep = rows + 6
    base = (lat * rows).astype(jnp.float32)

    def latitude(begin, count):
        at = lax.broadcasted_iota(jnp.int32, (count, layers, span), 0).astype(jnp.float32)
        return 2.0 * ((base + (at + begin)) + 0.5) / total - 1.0

    level = lax.broadcasted_iota(jnp.int32, (1, layers, span), 1)
    wet = (level.astype(jnp.float32) < depth[...]).astype(jnp.float32)
    wet_e = wet * to_east(wet)
    wet_n = wet[:-1] * wet[1:]
    u = st[:, 0:layers, :]
    v = st[:, layers : 2 * layers, :]
    h = st[:, 2 * layers : 3 * layers, :]
    warm = st[:, 3 * layers : 4 * layers, :]
    salt = st[:, 4 * layers : 5 * layers, :]

    def inner(a):
        return a[1 : deep - 1]

    def laplace(a, low, high):
        block, eface = a[low:high], wet_e[low:high]
        fe = eface * (to_east(block) - block)
        fn = wet_n[low - 1 : high] * (a[low : high + 1] - a[low - 1 : high])
        return fe - to_west(fe) + fn[1:] - fn[:-1]

    dens = salt_coef * salt - heat_coef * warm
    press = gravity * h + dens
    cor = coriolis_coef * latitude(-2.0, deep - 2)
    new_u = inner(wet_e) * (
        inner(u)
        + cor * inner(v)
        - (to_east(inner(press)) - inner(press))
        + viscosity * laplace(u, 1, deep - 1)
    )
    new_v = wet_n[1:] * (
        inner(v)
        - cor * inner(u)
        - (press[2:] - inner(press))
        + viscosity * laplace(v, 1, deep - 1)
    )
    q_e = inner(wet_e * u * 0.5 * (h + to_east(h)))
    q_n = wet_n * v[:-1] * 0.5 * (h[:-1] + h[1:])
    new_h = inner(wet) * (inner(h) - (q_e - to_west(q_e) + q_n[1:] - q_n[:-1]))
    dens = inner(dens)
    below = jnp.where(level < layers - 1, pltpu.roll(dens, layers - 1, 1) - dens, 0.0)
    kappa = inner(wet) * (kappa_base + kappa_var / (1.0 + 10.0 * below * below))

    def upwind(flow, spread):
        return jnp.maximum(flow, 0.0) + spread, jnp.minimum(flow, 0.0) - spread

    he, ke = new_h[1:-1], kappa[1:-1]
    face_e, face_n = wet_e[2:-2], wet_n[1:-1]
    a_e, b_e = upwind(
        face_e * new_u[1:-1] * 0.5 * (he + to_east(he)), face_e * 0.5 * (ke + to_east(ke))
    )
    a_n, b_n = upwind(
        face_n * new_v[:-1] * 0.5 * (new_h[:-1] + new_h[1:]),
        face_n * 0.5 * (kappa[:-1] + kappa[1:]),
    )
    sub = 1.0 / NSUB
    a_w, b_w = to_west(a_e), to_west(b_e)
    coef[0] = 1.0 - sub * (a_e - b_w + a_n[1:] - b_n[:-1])
    coef[1] = -sub * b_e
    coef[2] = sub * a_w
    coef[3] = -sub * b_n[1:]
    coef[4] = sub * a_n[:-1]
    wet_in = wet[2:-2]
    wets[...] = wet_in

    chl = tr[1 : rows + 3, layers : 2 * layers, :]
    att = wet_in * (water_att + chlorophyll_att * chl * chl)
    summed = att
    step = 1
    while step < layers:
        summed = summed + jnp.where(level >= step, pltpu.roll(summed, step, 1), 0.0)
        step *= 2
    lat_in = latitude(-1.0, rows + 2)
    top = (1.0 - 0.8 * lat_in * lat_in) * jnp.exp(att - summed)
    glow[...] = grow[2 : rows + 4] * top
    light = (top * (1.0 - jnp.exp(-att)))[1:-1, :, 0:cols]
    mine = wet[3:-3, :, 0:cols]
    mixed_t = (
        mine * (warm[3:-3] + tracer_diff * laplace(warm, 3, deep - 3))[:, :, 0:cols]
        + heat_gain * light
    )
    mixed_s = mine * (salt[3:-3] + tracer_diff * laplace(salt, 3, deep - 3))[:, :, 0:cols]
    for row in range(rows):
        pick = pl.ds(row, layers, stride=rows)
        later = pl.ds(layers * rows + row, layers, stride=rows)
        out_vel[pick, :] = new_u[2 + row, :, 0:cols]
        out_vel[later, :] = new_v[2 + row, :, 0:cols]
        out_thick[pick, :] = new_h[2 + row, :, 0:cols]
        out_hydro[pick, :] = mixed_t[row]
        out_hydro[later, :] = mixed_s[row]
        out_abs[pick, :] = light[row]

    def advance(src, at, width):
        c = src[at + 1].reshape(ntr, layers, span)
        up = src[at + 2].reshape(ntr, layers, span)[:, :, 0:width]
        down = src[at].reshape(ntr, layers, span)[:, :, 0:width]
        return c, up, down

    def finish(src, at, face, width):
        c, up, down = advance(src, at, width)
        k = [coef[i, face, :, 0:width] for i in range(5)]
        adv = (
            k[0] * c[:, :, 0:width]
            + k[1] * to_east(c)[:, :, 0:width]
            + k[2] * to_west(c)[:, :, 0:width]
            + k[3] * up
            + k[4] * down
        )
        flat = adv.reshape(fields, width)
        hi = flat.astype(jnp.bfloat16)
        lo = (flat - hi.astype(jnp.float32)).astype(jnp.bfloat16)

        def mul(a, b):
            return jnp.dot(a, b, preferred_element_type=jnp.float32)

        new = flat + (mul(couple_hi, hi) + (mul(couple_hi, lo) + mul(couple_lo, hi)))
        nut, plk = adv[0], adv[1]
        uptake = glow[face, :, 0:width] * plk * nut * nut / (1.0 + nut * nut)
        new = new.reshape(ntr, layers, width)
        w = wets[face, :, 0:width]
        first_two = (
            w * (new[0] - sub * uptake),
            w * (new[1] + sub * uptake),
        )
        return (w * new).reshape(fields, width), first_two

    def first_step(at):
        new, (zero, one) = finish(tr, at, at, span)
        mid[at] = new
        mid[at, 0:layers, :] = zero
        mid[at, layers : 2 * layers, :] = one

    for at in range(rows + 2):
        first_step(at)
    for row in range(rows):
        new, (zero, one) = finish(mid, row, row + 1, cols)
        out_tr[pl.ds(row, fields, stride=rows), :] = new
        out_tr[pl.ds(row, layers, stride=rows), :] = zero
        out_tr[pl.ds(layers * rows + row, layers, stride=rows), :] = one


def per_device(
    velocity,
    thickness,
    hydrography,
    tracers,
    land_mask,
    bottom_layer,
    row_biome,
    reaction_rates,
    growth_rates,
):
    ntr, layers, rows, cols = tracers.shape
    lats, lons = lax.axis_size("lat"), lax.axis_size("lon")
    state, fields = 5 * layers, ntr * layers
    near = state + fields + 4 * layers + 2 * rows
    whole = near + fields + 2 * layers
    sides = 1 if lons <= 2 else 2
    sizes = (lats, lons, layers, rows, cols, growth_rates.shape[0], near, sides)
    flat = [a.reshape(-1, cols) for a in (velocity, thickness, hydrography, tracers)]
    vmem = pl.BlockSpec(memory_space=pltpu.VMEM)
    smem = pl.BlockSpec(memory_space=pltpu.SMEM)
    hbm = pl.BlockSpec(memory_space=pltpu.HBM)
    f32 = jnp.float32
    lon_shapes = [jax.ShapeDtypeStruct(a.shape, f32) for a in flat] + [
        jax.ShapeDtypeStruct((2 * rows, cols), f32),
        jax.ShapeDtypeStruct((2, near, cols), f32),
    ]
    got = pl.pallas_call(
        functools.partial(exchange, sizes),
        out_shape=[jax.ShapeDtypeStruct((2, whole, cols), f32)] + lon_shapes * sides,
        in_specs=[smem] * 2 + [hbm] * 6,
        out_specs=[pl.BlockSpec(memory_space=pl.ANY)] * (1 + 6 * sides),
        scratch_shapes=[
            pltpu.VMEM((2 * rows, cols), f32),
            pltpu.VMEM((2, whole, cols), f32),
            pltpu.SemaphoreType.DMA((2, 2)),
            pltpu.SemaphoreType.DMA((2, 2)),
            pltpu.SemaphoreType.DMA((2, 7)),
            pltpu.SemaphoreType.DMA((2, 7)),
            pltpu.SemaphoreType.DMA((6,)),
            *[pltpu.VMEM(a.shape, f32) for a in flat],
            pltpu.VMEM((rows, cols), jnp.int32),
            pltpu.VMEM((rows, cols), jnp.int32),
        ],
        compiler_params=pltpu.CompilerParams(
            collective_id=0, has_side_effects=True, vmem_limit_bytes=62 * 1024 * 1024
        ),
        name="exchange",
    )(row_biome, growth_rates, *flat, land_mask, bottom_layer)
    span = 2 * cols
    operands = [*flat, land_mask, bottom_layer, reaction_rates, *got]
    count = len(operands)
    outs = pl.pallas_call(
        functools.partial(load_all, functools.partial(compute, sizes), count),
        out_shape=[jax.ShapeDtypeStruct(flat[i].shape, f32) for i in (0, 1, 2, 3, 1)],
        in_specs=[smem] * 2 + [hbm] * count,
        out_specs=[vmem] * 5,
        scratch_shapes=[pltpu.VMEM(a.shape, a.dtype) for a in operands]
        + [
            pltpu.VMEM((2 * rows, cols), f32),
            pltpu.VMEM((rows + 6, state, span), f32),
            pltpu.VMEM((rows + 4, fields, span), f32),
            pltpu.VMEM((rows + 2, fields, span), f32),
            pltpu.VMEM((rows + 6, layers, span), f32),
            pltpu.VMEM((rows + 6, layers, span), f32),
            pltpu.VMEM((5, rows + 2, layers, span), f32),
            pltpu.VMEM((rows + 2, layers, span), f32),
            pltpu.VMEM((rows + 2, layers, span), f32),
            pltpu.SemaphoreType.DMA((count,)),
        ],
        compiler_params=pltpu.CompilerParams(vmem_limit_bytes=62 * 1024 * 1024),
        name="ocean_step",
    )(row_biome, growth_rates, *operands)
    return (
        outs[0].reshape(velocity.shape),
        outs[1].reshape(thickness.shape),
        outs[2].reshape(hydrography.shape),
        outs[3].reshape(tracers.shape),
        outs[4].reshape(thickness.shape),
    )


def solution(mesh):
    in_specs = (
        P(None, None, "lat", "lon"),
        P(None, "lat", "lon"),
        P(None, None, "lat", "lon"),
        P(None, None, "lat", "lon"),
        P("lat", "lon"),
        P("lat", "lon"),
        P("lat"),
        P(),
        P(),
    )
    out_specs = (
        P(None, None, "lat", "lon"),
        P(None, "lat", "lon"),
        P(None, None, "lat", "lon"),
        P(None, None, "lat", "lon"),
        P(None, "lat", "lon"),
    )
    return jax.shard_map(
        per_device, mesh=mesh, in_specs=in_specs, out_specs=out_specs, check_vma=False
    )
```

```python
import functools

import jax
import jax.numpy as jnp
from jax import lax
from jax.experimental import pallas as pl
from jax.experimental.pallas import tpu as pltpu
from jax.sharding import PartitionSpec as P

NSUB = 2
heat_coef = 0.2
salt_coef = 0.25
gravity = 0.3
viscosity = 0.1
coriolis_coef = 0.3
tracer_diff = 0.1
kappa_base = 0.02
kappa_var = 0.1
water_att = 0.1
chlorophyll_att = 0.2
heat_gain = 1.0
MESH = pl.DeviceIdType.MESH


def growth_of(biome, growth, row, kinds):
    value = jnp.float32(0.0)
    for kind in range(kinds):
        value = jnp.where(biome[row] == kind, growth[kind], value)
    return value


def write_misc(misc, land, bottom, biome, growth, rows, cols, kinds):
    misc[0:rows, :] = (land[...] * bottom[...]).astype(jnp.float32)
    for row in range(rows):
        misc[rows + row : rows + row + 1, :] = jnp.full(
            (1, cols), growth_of(biome, growth, row, kinds), jnp.float32
        )


def exchange(sizes, biome, growth, *refs):
    held, refs = refs[:6], refs[6:]
    lats, lons, layers, rows, cols, kinds, near, sides = sizes
    fields = held[3].shape[0] // rows
    got_ns = refs[0]
    got_lon = [refs[1 + 6 * i : 7 + 6 * i] for i in range(sides)]
    misc, pack, send_ns, recv_ns, send_lon, recv_lon, load_sem = refs[1 + 6 * sides : 8 + 6 * sides]
    local = refs[8 + 6 * sides :]
    vel, thick, hydro, tracers, land, bottom = local
    loads = [
        pltpu.make_async_copy(held[i], local[i], load_sem.at[i]) for i in (4, 5, 3, 0, 2, 1)
    ]
    for load in loads:
        load.start()
    lat, lon = lax.axis_index("lat"), lax.axis_index("lon")
    barrier = pltpu.get_barrier_semaphore()
    around = [
        (lat > 0, (lat - 1, lon)),
        (lat < lats - 1, (lat + 1, lon)),
        (lon > 0, (lat, lon - 1)),
        (lon < lons - 1, (lat, lon + 1)),
    ]
    for there, where in around:

        @pl.when(there)
        def _(where=where):
            pl.semaphore_signal(barrier, inc=1, device_id=where, device_id_type=MESH)

    def ns_copy(side, part):
        to = lat + 1 if side == 0 else lat - 1
        return pltpu.make_async_remote_copy(
            src_ref=pack.at[side, cuts[part] : cuts[part + 1]],
            dst_ref=got_ns.at[side, cuts[part] : cuts[part + 1]],
            send_sem=send_ns.at[side, part],
            recv_sem=recv_ns.at[side, part],
            device_id=(to, lon),
            device_id_type=MESH,
        )

    def lon_copy(way, item):
        slot = way if sides == 2 else 0
        to = lon + 1 if way == 0 else lon - 1
        if item < 5:
            src = (*held[:4], misc)[item]
            dst = got_lon[slot][item]
        else:
            src = got_ns.at[item - 5, 0:near]
            dst = got_lon[slot][5].at[item - 5]
        return pltpu.make_async_remote_copy(
            src_ref=src,
            dst_ref=dst,
            send_sem=send_lon.at[way, item],
            recv_sem=recv_lon.at[way, item],
            device_id=(lat, to),
            device_id_type=MESH,
        )

    cuts = (0, near, got_ns.shape[1])
    south, north = lat > 0, lat < lats - 1
    west, east = lon > 0, lon < lons - 1
    ns_send = (north, south)
    ns_recv = (south, north)
    lon_send = (east, west)
    lon_recv = (west, east)
    peers = sum(there.astype(jnp.int32) for there, _ in around)
    pl.semaphore_wait(barrier, peers)
    for way in range(2):

        @pl.when(lon_send[way])
        def _(way=way):
            for item in (3, 0, 2, 1):
                lon_copy(way, item).start()

    for load in loads[:2]:
        load.wait()
    write_misc(misc, land, bottom, biome, growth, rows, cols, kinds)
    for way in range(2):

        @pl.when(lon_send[way])
        def _(way=way):
            lon_copy(way, 4).start()

    for load in loads[2:]:
        load.wait()

    def state_row(side, start, row):
        for ref, count in ((vel, 2 * layers), (thick, layers), (hydro, 2 * layers)):
            pack[side, start : start + count, :] = ref[pl.ds(row, count, stride=rows), :]
            start += count

    def second_row(side, start, row):
        flow, one = 2 * layers, layers
        pack[side, start : start + flow, :] = vel[pl.ds(row, flow, stride=rows), :]
        pack[side, start + flow : start + flow + one, :] = thick[pl.ds(row, one, stride=rows), :]
        warm = hydro[pl.ds(row, one, stride=rows), :]
        salt = hydro[pl.ds(one * rows + row, one, stride=rows), :]
        pack[side, start + flow + one : start + flow + 2 * one, :] = (
            salt_coef * salt - heat_coef * warm
        )

    def third_row(side, start, row):
        one = layers
        pack[side, start : start + one, :] = vel[pl.ds(one * rows + row, one, stride=rows), :]
        pack[side, start + one : start + 2 * one, :] = thick[pl.ds(row, one, stride=rows), :]

    def tracer_row(side, start, row):
        pack[side, start : start + fields, :] = tracers[pl.ds(row, fields, stride=rows), :]

    state = 5 * layers
    order = ((rows - 1, rows - 2, rows - 3), (0, 1, 2))
    for side in range(2):
        state_row(side, 0, order[side][0])
        tracer_row(side, state, order[side][0])
        second_row(side, state + fields, order[side][1])
        pack[side, near - 2 * rows : near, :] = misc[...]

        @pl.when(ns_send[side])
        def _(side=side):
            ns_copy(side, 0).start()

    for side in range(2):
        tracer_row(side, near, order[side][1])
        third_row(side, near + fields, order[side][2])

        @pl.when(ns_send[side])
        def _(side=side):
            ns_copy(side, 1).start()

    for side in range(2):

        @pl.when(ns_recv[side])
        def _(side=side):
            ns_copy(side, 0).wait_recv()
            for way in range(2):

                @pl.when(lon_send[way])
                def _(way=way):
                    lon_copy(way, 5 + side).start()

    for way in range(2):

        @pl.when(lon_recv[way])
        def _(way=way):
            for item in range(5):
                lon_copy(way, item).wait_recv()
            for side in range(2):

                @pl.when(ns_recv[side])
                def _(side=side):
                    lon_copy(way, 5 + side).wait_recv()

        @pl.when(lon_send[way])
        def _(way=way):
            for item in range(5):
                lon_copy(way, item).wait_send()
            for side in range(2):

                @pl.when(ns_recv[side])
                def _(side=side):
                    lon_copy(way, 5 + side).wait_send()

    for side in range(2):

        @pl.when(ns_recv[side])
        def _(side=side):
            ns_copy(side, 1).wait_recv()

        @pl.when(ns_send[side])
        def _(side=side):
            ns_copy(side, 0).wait_send()
            ns_copy(side, 1).wait_send()


def to_east(values):
    return pltpu.roll(values, values.shape[-1] - 1, values.ndim - 1)


def to_west(values):
    return pltpu.roll(values, 1, values.ndim - 1)


def load_all(body, count, biome, growth, *refs):
    held, outs = refs[:count], refs[count : count + 5]
    local, rest, sems = refs[count + 5 : 2 * count + 5], refs[2 * count + 5 : -1], refs[-1]
    loads = [pltpu.make_async_copy(held[i], local[i], sems.at[i]) for i in range(count)]
    for load in loads:
        load.start()
    body(loads, biome, growth, *local, *outs, *rest)


def compute(sizes, loads, biome, growth, vel, thick, hydro, tracers, land, bottom, rates, *refs):
    lats, lons, layers, rows, cols, kinds, near, sides = sizes
    fields = tracers.shape[0] // rows
    ntr = fields // layers
    got_ns = refs[0]
    got_lon = [refs[1 + 6 * i : 7 + 6 * i] for i in range(sides)]
    out_vel, out_thick, out_hydro, out_tr, out_abs = refs[1 + 6 * sides : 6 + 6 * sides]
    misc, st, tr, mid, depth, grow, coef, glow, wets = refs[6 + 6 * sides :]
    lat, lon = lax.axis_index("lat"), lax.axis_index("lon")
    span = 2 * cols
    state = 5 * layers
    for load in loads[:7]:
        load.wait()
    write_misc(misc, land, bottom, biome, growth, rows, cols, kinds)
    for row in range(rows):
        start = 0
        for ref, count in ((vel, 2 * layers), (thick, layers), (hydro, 2 * layers)):
            st[3 + row, start : start + count, 0:cols] = ref[pl.ds(row, count, stride=rows), :]
            start += count
        tr[2 + row, :, 0:cols] = tracers[pl.ds(row, fields, stride=rows), :]

    lanes = lax.broadcasted_iota(jnp.int32, (1, cols), 1)
    first = lanes < cols // 2
    lane_e = jnp.logical_and(first, lon < lons - 1)
    lane_w = jnp.logical_and(jnp.logical_not(first), lon > 0)

    def beside(load, mask=None):
        west_part = load(got_lon[0])
        east_part = load(got_lon[-1])
        use_e, use_w = lane_e, lane_w
        if mask is not None:
            use_e, use_w = jnp.logical_and(use_e, mask), jnp.logical_and(use_w, mask)
        return jnp.where(use_e, east_part, jnp.where(use_w, west_part, 0.0))

    def both(ref, at, start, own, side_values):
        count = own.shape[0]
        ref[at, start : start + count, 0:cols] = own
        ref[at, start : start + count, cols:span] = side_values

    wide = lax.broadcasted_iota(jnp.int32, (fields, ntr), 0) // layers
    pick_t = (wide == lax.broadcasted_iota(jnp.int32, (fields, ntr), 1)).astype(jnp.float32)
    spread_rates = jnp.dot(
        pick_t,
        lax.dot_general(
            rates[...],
            pick_t,
            (((1,), (1,)), ((), ())),
            precision=lax.Precision.HIGHEST,
            preferred_element_type=jnp.float32,
        ),
        precision=lax.Precision.HIGHEST,
        preferred_element_type=jnp.float32,
    )
    same = (
        lax.broadcasted_iota(jnp.int32, (fields, fields), 0) % layers
        == lax.broadcasted_iota(jnp.int32, (fields, fields), 1) % layers
    )
    couple = jnp.where(same, spread_rates / NSUB, 0.0)
    couple_hi = couple.astype(jnp.bfloat16)
    couple_lo = (couple - couple_hi.astype(jnp.float32)).astype(jnp.bfloat16)

    for load in loads[7:]:
        load.wait()
    for row in range(rows):
        start = 0
        for item, count in enumerate((2 * layers, layers, 2 * layers)):
            pick = pl.ds(row, count, stride=rows)
            st[3 + row, start : start + count, cols:span] = beside(
                lambda got, i=item, p=pick: got[i][p, :]
            )
            start += count
        pick = pl.ds(row, fields, stride=rows)
        tr[2 + row, :, cols:span] = beside(lambda got, p=pick: got[3][p, :])
    for ref, begin in ((depth, 0), (grow, rows)):
        for row in range(rows):
            pick = slice(begin + row, begin + row + 1)
            ref[3 + row, :, 0:cols] = jnp.broadcast_to(misc[pick, :], (layers, cols))
            ref[3 + row, :, cols:span] = jnp.broadcast_to(
                beside(lambda got, p=pick: got[4][p, :]), (layers, cols)
            )
    for side in range(2):
        there = lat > 0 if side == 0 else lat < lats - 1
        mask = jnp.logical_and(lanes >= 0, there)

        def own_part(begin, count, side=side, mask=mask):
            return jnp.where(mask, got_ns[side, begin : begin + count, :], 0.0)

        def far_part(begin, count, side=side, mask=mask):
            return beside(lambda got: got[5][side, begin : begin + count, :], mask)

        place = (2, 1, 0) if side == 0 else (rows + 3, rows + 4, rows + 5)
        place_tr = (1, 0) if side == 0 else (rows + 2, rows + 3)
        source = (rows - 1, rows - 2, rows - 3) if side == 0 else (0, 1, 2)
        both(st, place[0], 0, own_part(0, state), far_part(0, state))
        both(tr, place_tr[0], 0, own_part(state, fields), far_part(state, fields))
        both(
            st,
            place[1],
            0,
            own_part(state + fields, 3 * layers),
            far_part(state + fields, 3 * layers),
        )
        empty = jnp.zeros((layers, cols), jnp.float32)
        at = state + fields + 3 * layers
        both(st, place[1], 3 * layers, empty, empty)
        scale = 1.0 / salt_coef
        both(
            st, place[1], 4 * layers, scale * own_part(at, layers), scale * far_part(at, layers)
        )
        both(tr, place_tr[1], 0, own_part(near, fields), jnp.zeros((fields, cols), jnp.float32))
        nothing = jnp.zeros((state, cols), jnp.float32)
        both(st, place[2], 0, nothing, nothing)
        st[place[2], layers : 3 * layers, 0:cols] = own_part(near + fields, 2 * layers)
        begin = near - 2 * rows
        for ref, extra in ((depth, 0), (grow, rows)):
            for step in range(3):
                at = begin + extra + source[step]
                ref[place[step], :, 0:cols] = jnp.broadcast_to(own_part(at, 1), (layers, cols))
                ref[place[step], :, cols:span] = jnp.broadcast_to(far_part(at, 1), (layers, cols))

    total = rows * lats
    deep = rows + 6
    base = (lat * rows).astype(jnp.float32)

    def latitude(begin, count):
        at = lax.broadcasted_iota(jnp.int32, (count, layers, span), 0).astype(jnp.float32)
        return 2.0 * ((base + (at + begin)) + 0.5) / total - 1.0

    level = lax.broadcasted_iota(jnp.int32, (1, layers, span), 1)
    wet = (level.astype(jnp.float32) < depth[...]).astype(jnp.float32)
    wet_e = wet * to_east(wet)
    wet_n = wet[:-1] * wet[1:]
    u = st[:, 0:layers, :]
    v = st[:, layers : 2 * layers, :]
    h = st[:, 2 * layers : 3 * layers, :]
    warm = st[:, 3 * layers : 4 * layers, :]
    salt = st[:, 4 * layers : 5 * layers, :]

    def inner(a):
        return a[1 : deep - 1]

    def laplace(a, low, high):
        block, eface = a[low:high], wet_e[low:high]
        fe = eface * (to_east(block) - block)
        fn = wet_n[low - 1 : high] * (a[low : high + 1] - a[low - 1 : high])
        return fe - to_west(fe) + fn[1:] - fn[:-1]

    dens = salt_coef * salt - heat_coef * warm
    press = gravity * h + dens
    cor = coriolis_coef * latitude(-2.0, deep - 2)
    new_u = inner(wet_e) * (
        inner(u)
        + cor * inner(v)
        - (to_east(inner(press)) - inner(press))
        + viscosity * laplace(u, 1, deep - 1)
    )
    new_v = wet_n[1:] * (
        inner(v)
        - cor * inner(u)
        - (press[2:] - inner(press))
        + viscosity * laplace(v, 1, deep - 1)
    )
    q_e = inner(wet_e * u * 0.5 * (h + to_east(h)))
    q_n = wet_n * v[:-1] * 0.5 * (h[:-1] + h[1:])
    new_h = inner(wet) * (inner(h) - (q_e - to_west(q_e) + q_n[1:] - q_n[:-1]))
    dens = inner(dens)
    below = jnp.where(level < layers - 1, pltpu.roll(dens, layers - 1, 1) - dens, 0.0)
    kappa = inner(wet) * (kappa_base + kappa_var / (1.0 + 10.0 * below * below))

    def upwind(flow, spread):
        return jnp.maximum(flow, 0.0) + spread, jnp.minimum(flow, 0.0) - spread

    he, ke = new_h[1:-1], kappa[1:-1]
    face_e, face_n = wet_e[2:-2], wet_n[1:-1]
    a_e, b_e = upwind(
        face_e * new_u[1:-1] * 0.5 * (he + to_east(he)), face_e * 0.5 * (ke + to_east(ke))
    )
    a_n, b_n = upwind(
        face_n * new_v[:-1] * 0.5 * (new_h[:-1] + new_h[1:]),
        face_n * 0.5 * (kappa[:-1] + kappa[1:]),
    )
    sub = 1.0 / NSUB
    a_w, b_w = to_west(a_e), to_west(b_e)
    coef[0] = 1.0 - sub * (a_e - b_w + a_n[1:] - b_n[:-1])
    coef[1] = -sub * b_e
    coef[2] = sub * a_w
    coef[3] = -sub * b_n[1:]
    coef[4] = sub * a_n[:-1]
    wet_in = wet[2:-2]
    wets[...] = wet_in

    chl = tr[1 : rows + 3, layers : 2 * layers, :]
    att = wet_in * (water_att + chlorophyll_att * chl * chl)
    summed = att
    step = 1
    while step < layers:
        summed = summed + jnp.where(level >= step, pltpu.roll(summed, step, 1), 0.0)
        step *= 2
    lat_in = latitude(-1.0, rows + 2)
    top = (1.0 - 0.8 * lat_in * lat_in) * jnp.exp(att - summed)
    glow[...] = grow[2 : rows + 4] * top
    light = (top * (1.0 - jnp.exp(-att)))[1:-1, :, 0:cols]
    mine = wet[3:-3, :, 0:cols]
    mixed_t = (
        mine * (warm[3:-3] + tracer_diff * laplace(warm, 3, deep - 3))[:, :, 0:cols]
        + heat_gain * light
    )
    mixed_s = mine * (salt[3:-3] + tracer_diff * laplace(salt, 3, deep - 3))[:, :, 0:cols]
    for row in range(rows):
        pick = pl.ds(row, layers, stride=rows)
        later = pl.ds(layers * rows + row, layers, stride=rows)
        out_vel[pick, :] = new_u[2 + row, :, 0:cols]
        out_vel[later, :] = new_v[2 + row, :, 0:cols]
        out_thick[pick, :] = new_h[2 + row, :, 0:cols]
        out_hydro[pick, :] = mixed_t[row]
        out_hydro[later, :] = mixed_s[row]
        out_abs[pick, :] = light[row]

    def advance(src, at, width):
        c = src[at + 1].reshape(ntr, layers, span)
        up = src[at + 2].reshape(ntr, layers, span)[:, :, 0:width]
        down = src[at].reshape(ntr, layers, span)[:, :, 0:width]
        return c, up, down

    def finish(src, at, face, width):
        c, up, down = advance(src, at, width)
        k = [coef[i, face, :, 0:width] for i in range(5)]
        adv = (
            k[0] * c[:, :, 0:width]
            + k[1] * to_east(c)[:, :, 0:width]
            + k[2] * to_west(c)[:, :, 0:width]
            + k[3] * up
            + k[4] * down
        )
        flat = adv.reshape(fields, width)
        hi = flat.astype(jnp.bfloat16)
        lo = (flat - hi.astype(jnp.float32)).astype(jnp.bfloat16)

        def mul(a, b):
            return jnp.dot(a, b, preferred_element_type=jnp.float32)

        new = flat + (mul(couple_hi, hi) + (mul(couple_hi, lo) + mul(couple_lo, hi)))
        nut, plk = adv[0], adv[1]
        uptake = glow[face, :, 0:width] * plk * nut * nut / (1.0 + nut * nut)
        new = new.reshape(ntr, layers, width)
        w = wets[face, :, 0:width]
        first_two = (
            w * (new[0] - sub * uptake),
            w * (new[1] + sub * uptake),
        )
        return (w * new).reshape(fields, width), first_two

    def first_step(at):
        new, (zero, one) = finish(tr, at, at, span)
        mid[at] = new
        mid[at, 0:layers, :] = zero
        mid[at, layers : 2 * layers, :] = one

    for at in range(rows + 2):
        first_step(at)
    for row in range(rows):
        new, (zero, one) = finish(mid, row, row + 1, cols)
        out_tr[pl.ds(row, fields, stride=rows), :] = new
        out_tr[pl.ds(row, layers, stride=rows), :] = zero
        out_tr[pl.ds(layers * rows + row, layers, stride=rows), :] = one


def per_device(
    velocity,
    thickness,
    hydrography,
    tracers,
    land_mask,
    bottom_layer,
    row_biome,
    reaction_rates,
    growth_rates,
):
    ntr, layers, rows, cols = tracers.shape
    lats, lons = lax.axis_size("lat"), lax.axis_size("lon")
    state, fields = 5 * layers, ntr * layers
    near = state + fields + 4 * layers + 2 * rows
    whole = near + fields + 2 * layers
    sides = 1 if lons <= 2 else 2
    sizes = (lats, lons, layers, rows, cols, growth_rates.shape[0], near, sides)
    flat = [a.reshape(-1, cols) for a in (velocity, thickness, hydrography, tracers)]
    vmem = pl.BlockSpec(memory_space=pltpu.VMEM)
    smem = pl.BlockSpec(memory_space=pltpu.SMEM)
    hbm = pl.BlockSpec(memory_space=pltpu.HBM)
    f32 = jnp.float32
    lon_shapes = [jax.ShapeDtypeStruct(a.shape, f32) for a in flat] + [
        jax.ShapeDtypeStruct((2 * rows, cols), f32),
        jax.ShapeDtypeStruct((2, near, cols), f32),
    ]
    got = pl.pallas_call(
        functools.partial(exchange, sizes),
        out_shape=[jax.ShapeDtypeStruct((2, whole, cols), f32)] + lon_shapes * sides,
        in_specs=[smem] * 2 + [hbm] * 6,
        out_specs=[pl.BlockSpec(memory_space=pl.ANY)] * (1 + 6 * sides),
        scratch_shapes=[
            pltpu.VMEM((2 * rows, cols), f32),
            pltpu.VMEM((2, whole, cols), f32),
            pltpu.SemaphoreType.DMA((2, 2)),
            pltpu.SemaphoreType.DMA((2, 2)),
            pltpu.SemaphoreType.DMA((2, 7)),
            pltpu.SemaphoreType.DMA((2, 7)),
            pltpu.SemaphoreType.DMA((6,)),
            *[pltpu.VMEM(a.shape, f32) for a in flat],
            pltpu.VMEM((rows, cols), jnp.int32),
            pltpu.VMEM((rows, cols), jnp.int32),
        ],
        compiler_params=pltpu.CompilerParams(
            collective_id=0, has_side_effects=True, vmem_limit_bytes=62 * 1024 * 1024
        ),
        name="exchange",
    )(row_biome, growth_rates, *flat, land_mask, bottom_layer)
    span = 2 * cols
    operands = [*flat, land_mask, bottom_layer, reaction_rates, *got]
    count = len(operands)
    outs = pl.pallas_call(
        functools.partial(load_all, functools.partial(compute, sizes), count),
        out_shape=[jax.ShapeDtypeStruct(flat[i].shape, f32) for i in (0, 1, 2, 3, 1)],
        in_specs=[smem] * 2 + [hbm] * count,
        out_specs=[vmem] * 5,
        scratch_shapes=[pltpu.VMEM(a.shape, a.dtype) for a in operands]
        + [
            pltpu.VMEM((2 * rows, cols), f32),
            pltpu.VMEM((rows + 6, state, span), f32),
            pltpu.VMEM((rows + 4, fields, span), f32),
            pltpu.VMEM((rows + 2, fields, span), f32),
            pltpu.VMEM((rows + 6, layers, span), f32),
            pltpu.VMEM((rows + 6, layers, span), f32),
            pltpu.VMEM((5, rows + 2, layers, span), f32),
            pltpu.VMEM((rows + 2, layers, span), f32),
            pltpu.VMEM((rows + 2, layers, span), f32),
            pltpu.SemaphoreType.DMA((count,)),
        ],
        compiler_params=pltpu.CompilerParams(vmem_limit_bytes=62 * 1024 * 1024),
        name="ocean_step",
    )(row_biome, growth_rates, *operands)
    return (
        outs[0].reshape(velocity.shape),
        outs[1].reshape(thickness.shape),
        outs[2].reshape(hydrography.shape),
        outs[3].reshape(tracers.shape),
        outs[4].reshape(thickness.shape),
    )


def solution(mesh):
    in_specs = (
        P(None, None, "lat", "lon"),
        P(None, "lat", "lon"),
        P(None, None, "lat", "lon"),
        P(None, None, "lat", "lon"),
        P("lat", "lon"),
        P("lat", "lon"),
        P("lat"),
        P(),
        P(),
    )
    out_specs = (
        P(None, None, "lat", "lon"),
        P(None, "lat", "lon"),
        P(None, None, "lat", "lon"),
        P(None, None, "lat", "lon"),
        P(None, "lat", "lon"),
    )
    return jax.shard_map(
        per_device, mesh=mesh, in_specs=in_specs, out_specs=out_specs, check_vma=False
    )
```
